32 devices in a mesh: row: 4 (over x, core), col: 8 (over z, y).
Axes of the slice: x: 2, y: 2, z: 4, core: 2. Of those that a mesh axis runs over, the one named last changes fastest.
Arguments:
- coefs: bfloat16 [1024, 4096], P('col', 'row'), may hold values from -6 to 6
- direction: bfloat16 [1024, 4096], P('col', 'row'), may hold values from -6 to 6
- tiles: bfloat16 [4, 192, 4096], P('row', 'col'), may hold values from -0.3125 to 0.3125
- block_rows: int32 [4, 192], P('row', 'col'), may hold values from 0 to 15
- block_cols: int32 [4, 192], P('row', 'col'), may hold values from 0 to 63
- counts: int32 [4, 8], P('row', 'col'), may hold values from 3 to 24, as said below
Outputs:
- h_coefs: bfloat16 [1024, 4096], P('col', 'row')
- h_direction: bfloat16 [1024, 4096], P('col', 'row')
The draws below stay inside these ranges and needn't reach their ends.
Inputs may be any that keep to these rules, and one draw needn't show every extreme that they name: `counts`: each value lies between 3 and 24; some device's list is full in every draw. `block_cols`: tiles of one device may repeat a place.
All inputs are finite; a program needn't handle non-finite values.
Results may differ from the reference program's by a relative error of at most 0.008.
Values may be sent and summed in bfloat16 or wider, within the bound.
A program may use at most 128 MiB of HBM per device.

```python
import jax
import jax.numpy as jnp
from jax import lax

BLOCK = 64
ORBS = 1024
RB_DEV = 16
TILES_DEV = 24
NB = 64
NBASIS = 4096
N_ROW = 4
N_COL = 8


def draw_counts(key, part):
    first_key, second_key = jax.random.split(jax.random.fold_in(key, 7))
    lowest = max(1, TILES_DEV // 8)
    values = jax.random.randint(first_key, (N_ROW * N_COL,), lowest, TILES_DEV + 1)
    chosen = jax.random.randint(second_key, (), 0, N_ROW * N_COL)
    values = jnp.where(jnp.arange(N_ROW * N_COL) == chosen, TILES_DEV, values)
    return values.reshape(N_ROW, N_COL).astype(jnp.int32)


def with_ends(array, rng, least, largest):
    spot = [jax.random.randint(jax.random.fold_in(rng, axis), (), 0, length) for axis, length in enumerate(array.shape)]
    longest = array.shape.index(max(array.shape))
    next_to = spot[:longest] + [(spot[longest] + 1) % array.shape[longest]] + spot[longest + 1:]
    return array.at[tuple(spot)].set(least).at[tuple(next_to)].set(largest)


def steps_of(own_key, shape, cuts, smallest, high):
    factor_of, own = 1.0, jax.random.fold_in(own_key, 6)
    for position, blocks in cuts:
        steps = jnp.exp(jax.random.uniform(jax.random.fold_in(own, position), (blocks,), jnp.float32, smallest / len(cuts), high / len(cuts)))
        factor_of = factor_of * jnp.repeat(steps, shape[position] // blocks).reshape([-1 if axis == position else 1 for axis in range(len(shape))])
    return factor_of


def centred(own_key, dims, deviation, bound, cuts=(), kind=jnp.bfloat16):
    array = deviation * jax.random.normal(own_key, dims, jnp.float32)
    if cuts:
        array = array * steps_of(own_key, dims, cuts, -0.22, 0.18)
    return jnp.clip(array, -bound, bound).astype(kind)


def setup_inputs(seed: int = 0) -> dict:
    seeds = jax.random.split(jax.random.key(seed), 7)
    coefs = centred(seeds[0], (ORBS, NBASIS), 1.0, 6.0, ((0, 8), (1, 4)))
    direction = centred(seeds[1], (ORBS, NBASIS), 1.0, 6.0, ((0, 8), (1, 4)))
    tiles = centred(seeds[2], (N_ROW, N_COL * TILES_DEV, BLOCK * BLOCK), (BLOCK * N_COL * TILES_DEV // RB_DEV // 2) ** -0.5, 0.3125, ((0, 4), (1, 8)))
    block_rows = with_ends(jax.random.randint(seeds[3], (N_ROW, N_COL * TILES_DEV), 0, RB_DEV), jax.random.fold_in(seeds[3], 1), 0, RB_DEV - 1).astype(jnp.int32)
    block_cols = with_ends(jax.random.randint(seeds[4], (N_ROW, N_COL * TILES_DEV), 0, NB), jax.random.fold_in(seeds[4], 1), 0, NB - 1).astype(jnp.int32)
    counts = draw_counts(jax.random.fold_in(seeds[6], 71), 0)
    return {"coefs": coefs, "direction": direction, "tiles": tiles, "block_rows": block_rows, "block_cols": block_cols, "counts": counts}


def reference(coefs, direction, tiles, block_rows, block_cols, counts):
    nblocks = RB_DEV * N_ROW
    panels = jnp.stack([coefs, direction]).astype(jnp.float32).reshape(2, ORBS, nblocks, BLOCK)
    slot = jnp.arange(N_COL * TILES_DEV, dtype=jnp.int32)
    owner = slot // TILES_DEV
    within = slot % TILES_DEV
    targets = jnp.arange(RB_DEV, dtype=jnp.int32)

    def group(r):
        valid = within < counts[r][owner]
        mats = jnp.where(valid[:, None], tiles[r].astype(jnp.float32), jnp.float32(0.0))
        mats = mats.reshape(N_COL, TILES_DEV, BLOCK, BLOCK)
        rows_here = block_rows[r].reshape(N_COL, TILES_DEV)
        cols_here = block_cols[r].reshape(N_COL, TILES_DEV)

        def step(total, pieces):
            tile_mats, tile_rows, tile_cols = pieces
            picked = jnp.take(panels, tile_cols, axis=2)
            contrib = jnp.einsum('pij,sopj->psoi', tile_mats, picked).reshape(TILES_DEV, -1)
            onehot = (tile_rows[:, None] == targets[None, :]).astype(jnp.float32)
            return total + jnp.dot(onehot.T, contrib, precision=lax.Precision.HIGHEST, preferred_element_type=jnp.float32), None

        start = jnp.zeros((RB_DEV, 2 * ORBS * BLOCK), jnp.float32)
        total, unused = lax.scan(step, start, (mats, rows_here, cols_here))
        return total

    totals = lax.map(group, jnp.arange(N_ROW, dtype=jnp.int32))
    totals = totals.reshape(N_ROW, RB_DEV, 2, ORBS, BLOCK).transpose(2, 3, 0, 1, 4)
    result = totals.reshape(2, ORBS, nblocks * BLOCK).astype(jnp.bfloat16)
    return result[0], result[1]
```

```python
import functools

import jax
import jax.numpy as jnp
from jax import lax
from jax.experimental import pallas as pl
from jax.experimental.pallas import tpu as pltpu
from jax.sharding import PartitionSpec as P

BLOCK = 64
X_CHUNKS = 4
HALVES = 2
P_SLOTS = 5
MESH = pl.DeviceIdType.MESH


def kernel(n_row, n_col, coef, direc, tiles, rows, cols, counts, out_c, out_d,
           xall, tall, mall, smeta, pbuf, gbuf, acc,
           sib_s, sib_r, cross_s, cross_r, fwd_s, fwd_r, ring_s, ring_r, meta_s, meta_r, loc):
    orbs, basis = coef.shape
    width = 2 * orbs
    slots = rows.shape[1]
    blocks = basis // BLOCK
    half_rows = BLOCK // HALVES
    chips = n_row // 2
    steps = n_col // 2
    part = basis // X_CHUNKS
    per = part // BLOCK

    me_r, me_c = lax.axis_index("row"), lax.axis_index("col")
    chip, core = me_r // 2, me_r % 2
    sibling = chip * 2 + 1 - core
    turn = me_c % 2
    pos = me_c // 2 + turn * (n_col - 1 - 2 * (me_c // 2))

    def at_pos(p):
        side = p // steps
        return 2 * (p + side * (n_col - 1 - 2 * p)) + side

    nxt, prv = at_pos((pos + 1) % n_col), at_pos((pos + n_col - 1) % n_col)

    barrier = pltpu.get_barrier_semaphore()
    for c in (nxt, prv):
        pl.semaphore_signal(barrier, inc=1, device_id=(me_r, c), device_id_type=MESH)
    pl.semaphore_signal(barrier, inc=1, device_id=(sibling, me_c), device_id_type=MESH)
    for k in range(1, chips):
        pl.semaphore_signal(barrier, inc=1, device_id=(((chip + k) % chips) * 2 + core, me_c), device_id_type=MESH)

    ids = lax.broadcasted_iota(jnp.int32, (1, slots), 1)
    mall[0, 0:1, 0:slots] = jnp.where(ids < counts[0, 0], rows[...], -1)
    mall[0, 1:2, 0:slots] = cols[...]
    tall[0] = tiles[...]
    base = me_r * blocks
    for c in range(X_CHUNKS):
        for a, src in enumerate((coef, direc)):
            piece = src[:, c * part:(c + 1) * part].astype(jnp.float32).T.astype(jnp.bfloat16)
            xall[pl.ds(base + c * per, per), :, a * orbs:(a + 1) * orbs] = piece.reshape(per, BLOCK, orbs)
    pl.semaphore_wait(barrier, 2 + 1 + chips - 1)

    def x_ref(owner, c):
        return xall.at[pl.ds(owner * blocks + c * per, per)]

    def x_copy(owner, c, to, send, recv):
        return pltpu.make_async_remote_copy(
            src_ref=x_ref(owner, c), dst_ref=x_ref(owner, c), send_sem=send, recv_sem=recv,
            device_id=(to, me_c), device_id_type=MESH)

    def cross_to(k, c):
        return x_copy(me_r, c, ((chip + k) % chips) * 2 + core, cross_s.at[k - 1, c], cross_r.at[k - 1, c])

    def cross_from(k, c):
        owner = ((chip + chips - k) % chips) * 2 + core
        return x_copy(owner, c, owner, cross_s.at[k - 1, c], cross_r.at[k - 1, c])

    def sib_to(c):
        return x_copy(me_r, c, sibling, sib_s.at[c], sib_r.at[c])

    def sib_from(c):
        return x_copy(sibling, c, sibling, sib_s.at[c], sib_r.at[c])

    def fwd_to(k, c):
        owner = ((chip + chips - k) % chips) * 2 + core
        return x_copy(owner, c, sibling, fwd_s.at[k - 1, c], fwd_r.at[k - 1, c])

    def fwd_from(k, c):
        owner = ((chip + chips - k) % chips) * 2 + 1 - core
        return x_copy(owner, c, sibling, fwd_s.at[k - 1, c], fwd_r.at[k - 1, c])

    def ring_slots(d, t):
        return (t - 1, t) if d == 0 else ((n_col - t + 1) % n_col, n_col - t)

    def ring(d, t, h):
        a, b = ring_slots(d, t)
        cut = pl.ds(h * half_rows, half_rows)
        return pltpu.make_async_remote_copy(
            src_ref=tall.at[a, cut], dst_ref=tall.at[b, cut],
            send_sem=ring_s.at[d, t - 1, h], recv_sem=ring_r.at[d, t - 1, h],
            device_id=(me_r, nxt if d == 0 else prv), device_id_type=MESH)

    def meta(d, t):
        a, b = ring_slots(d, t)
        return pltpu.make_async_remote_copy(
            src_ref=mall.at[a], dst_ref=mall.at[b],
            send_sem=meta_s.at[d, t - 1], recv_sem=meta_r.at[d, t - 1],
            device_id=(me_r, nxt if d == 0 else prv), device_id_type=MESH)

    def ring_parts(t):
        if t < steps:
            return [(d, h) for h in range(HALVES) for d in (0, 1)], (0, 1)
        return [(0, 0), (1, 1)], (0,)

    def to_smem(slot):
        copy = pltpu.make_async_copy(mall.at[slot], smeta.at[slot], loc.at[slot])
        copy.start()
        copy.wait()

    lane = lax.broadcasted_iota(jnp.int32, (16, 2 * BLOCK), 1)

    def slot_of(q):
        return (q % 2) * ((q + 1) // 2) + (1 - q % 2) * ((n_col - q // 2) % n_col)

    def build(q):
        slot, place = slot_of(q), q % P_SLOTS

        def pair(i, carry):
            at = pl.ds(pl.multiple_of(i * 2 * BLOCK, 2 * BLOCK), 2 * BLOCK)
            mats = tall[slot, :, at].reshape(BLOCK // 16, 16, 2 * BLOCK)
            target = jnp.where(lane < BLOCK, smeta[slot, 0, 2 * i], smeta[slot, 0, 2 * i + 1])
            for b in range(blocks):
                keep = jnp.where(target == b, 1.0, 0.0).astype(jnp.bfloat16)
                pbuf[place, b * BLOCK:(b + 1) * BLOCK, at] = (mats * keep[None]).reshape(BLOCK, 2 * BLOCK)
            return carry

        lax.fori_loop(0, slots // 2, pair, 0)

    def compute(q):
        slot, place = slot_of(q), q % P_SLOTS

        def pick(s, carry):
            gbuf[s] = xall[smeta[slot, 1, s]]
            return carry

        lax.fori_loop(0, slots, pick, 0, unroll=4)

        def strip(m, carry):
            at = pl.ds(pl.multiple_of(m * 256, 256), 256)
            acc[at, :] += jnp.dot(pbuf[place, at, :], gbuf[...].reshape(slots * BLOCK, width), preferred_element_type=jnp.float32)
            return carry

        lax.fori_loop(0, basis // 256, strip, 0)

    def send_ring(t):
        pieces, metas = ring_parts(t)
        for d in metas:
            meta(d, t).start()
        for d, h in pieces:
            ring(d, t, h).start()

    def ring_event(t):
        pieces, metas = ring_parts(t)
        more, more_metas = ring_parts(t + 1) if t < steps else ((), ())
        for d in metas:
            meta(d, t).wait_recv()
            if d in more_metas:
                meta(d, t + 1).start()
        for d, h in pieces:
            ring(d, t, h).wait_recv()
            if (d, h) in more:
                ring(d, t + 1, h).start()
        for d in metas:
            to_smem(ring_slots(d, t)[1])

    for c in range(X_CHUNKS):
        for k in range(1, chips):
            cross_to(k, c).start()
        if c == 0:
            send_ring(1)
    for c in range(X_CHUNKS):
        sib_to(c).start()
    to_smem(0)
    acc[...] = jnp.zeros_like(acc)
    build(0)

    events = [(((k - 1) * X_CHUNKS + c + 1) * 2.6, 0, k, c) for k in range(1, chips) for c in range(X_CHUNKS)]
    events += [(t * 3.9, 1, t, 0) for t in range(1, steps)]
    for _, kind, k, c in sorted(events):
        if kind == 0:
            cross_from(k, c).wait_recv()
            fwd_to(k, c).start()
        else:
            ring_event(k)
            for q in (2 * k - 1, 2 * k):
                if q < P_SLOTS:
                    build(q)
    for c in range(X_CHUNKS):
        sib_from(c).wait_recv()
    for k in range(1, chips):
        for c in range(X_CHUNKS):
            fwd_from(k, c).wait_recv()

    def early(q, carry):
        compute(q)
        return carry

    def late(q, carry):
        build(q)
        compute(q)
        return carry

    lax.fori_loop(0, P_SLOTS, early, 0)
    lax.fori_loop(P_SLOTS, n_col - 1, late, 0)
    ring_event(steps)
    lax.fori_loop(n_col - 1, n_col, late, 0)

    for a, out in enumerate((out_c, out_d)):
        for m in range(basis // 256):
            out[:, m * 256:(m + 1) * 256] = acc[m * 256:(m + 1) * 256, a * orbs:(a + 1) * orbs].T.astype(jnp.bfloat16)

    for c in range(X_CHUNKS):
        sib_to(c).wait_send()
        for k in range(1, chips):
            cross_to(k, c).wait_send()
            fwd_to(k, c).wait_send()
    for t in range(1, steps + 1):
        pieces, metas = ring_parts(t)
        for d in metas:
            meta(d, t).wait_send()
        for d, h in pieces:
            ring(d, t, h).wait_send()


def local(n_row, n_col, coefs, direction, tiles, block_rows, block_cols, counts):
    slots = tiles.shape[1]
    orbs, basis = coefs.shape
    width = 2 * orbs
    tile_mats = tiles[0].reshape(slots, BLOCK, BLOCK).transpose(1, 0, 2).reshape(BLOCK, slots * BLOCK)
    chips, steps = n_row // 2, n_col // 2
    vmem = pl.BlockSpec(memory_space=pltpu.VMEM)
    dma = pltpu.SemaphoreType.DMA
    out = jax.ShapeDtypeStruct((orbs, basis), jnp.bfloat16)
    return pl.pallas_call(
        functools.partial(kernel, n_row, n_col),
        out_shape=(out, out),
        in_specs=[vmem] * 5 + [pl.BlockSpec(memory_space=pltpu.SMEM)],
        out_specs=(vmem, vmem),
        scratch_shapes=[
            pltpu.VMEM((n_row * basis // BLOCK, BLOCK, width), jnp.bfloat16),
            pltpu.VMEM((n_col, BLOCK, slots * BLOCK), jnp.bfloat16),
            pltpu.VMEM((n_col, 8, 128), jnp.int32),
            pltpu.SMEM((n_col, 8, 128), jnp.int32),
            pltpu.VMEM((P_SLOTS, basis, slots * BLOCK), jnp.bfloat16),
            pltpu.VMEM((slots, BLOCK, width), jnp.bfloat16),
            pltpu.VMEM((basis, width), jnp.float32),
            dma((X_CHUNKS,)), dma((X_CHUNKS,)),
            dma((chips - 1, X_CHUNKS)), dma((chips - 1, X_CHUNKS)),
            dma((chips - 1, X_CHUNKS)), dma((chips - 1, X_CHUNKS)),
            dma((2, steps, HALVES)), dma((2, steps, HALVES)),
            dma((2, steps)), dma((2, steps)),
            dma((n_col,)),
        ],
        compiler_params=pltpu.CompilerParams(
            collective_id=0, has_side_effects=True, vmem_limit_bytes=56 * 2**20),
        name="block_sparse_apply",
    )(coefs, direction, tile_mats, block_rows, block_cols, counts)


def solution(mesh):
    body = functools.partial(local, mesh.shape["row"], mesh.shape["col"])
    return jax.shard_map(
        body,
        mesh=mesh,
        in_specs=(
            P("col", "row"),
            P("col", "row"),
            P("row", "col", None),
            P("row", "col"),
            P("row", "col"),
            P("row", "col"),
        ),
        out_specs=(P("col", "row"), P("col", "row")),
        check_vma=False,
    )
```

```python
import functools

import jax
import jax.numpy as jnp
from jax import lax
from jax.experimental import pallas as pl
from jax.experimental.pallas import tpu as pltpu
from jax.sharding import PartitionSpec as P

BLOCK = 64
X_CHUNKS = 4
HALVES = 2
MESH = pl.DeviceIdType.MESH


def kernel(n_row, n_col, coef, direc, tiles, rows, cols, counts, out_c, out_d,
           xall, tall, mall, smeta, sums, acc,
           sib_s, sib_r, cross_s, cross_r, fwd_s, fwd_r, ring_s, ring_r, meta_s, meta_r, loc):
    orbs, basis = coef.shape
    width = 2 * orbs
    slots = rows.shape[1]
    blocks = basis // BLOCK
    pairs = slots // 2
    cut_pairs = pairs // HALVES
    chips = n_row // 2
    steps = n_col // 2
    part = basis // X_CHUNKS
    per = part // BLOCK

    me_r, me_c = lax.axis_index("row"), lax.axis_index("col")
    chip, core = me_r // 2, me_r % 2
    sibling = chip * 2 + 1 - core
    turn = me_c % 2
    pos = me_c // 2 + turn * (n_col - 1 - 2 * (me_c // 2))

    def at_pos(p):
        side = p // steps
        return 2 * (p + side * (n_col - 1 - 2 * p)) + side

    nxt, prv = at_pos((pos + 1) % n_col), at_pos((pos + n_col - 1) % n_col)

    barrier = pltpu.get_barrier_semaphore()
    for c in (nxt, prv):
        pl.semaphore_signal(barrier, inc=1, device_id=(me_r, c), device_id_type=MESH)
    pl.semaphore_signal(barrier, inc=1, device_id=(sibling, me_c), device_id_type=MESH)
    for k in range(1, chips):
        pl.semaphore_signal(barrier, inc=1, device_id=(((chip + k) % chips) * 2 + core, me_c), device_id_type=MESH)

    lane1 = lax.broadcasted_iota(jnp.int32, (1, 128), 1)
    pad = lax.broadcasted_iota(jnp.int32, (8, 128), 0)
    row_key = jnp.where(lane1[:, :slots] < counts[0, 0], rows[...], blocks)
    mall[0] = jnp.zeros((8, 128), jnp.int32)
    mall[0, 0:1, 0:slots] = row_key * slots + lane1[:, :slots]
    mall[0, 1:2, 0:slots] = cols[...]
    mall[0, 2:3, 0:slots] = row_key
    wide = mall[0]
    tall_form = wide.T
    key_col, col_col, row_col = (tall_form[:slots, i:i + 1] for i in range(3))
    rank = jnp.sum((key_col < wide[0:1]).astype(jnp.int32), axis=0, keepdims=True)
    rank_col = jnp.where(pad == 0, rank, 0).T[:slots, 0:1]
    hit = rank_col == lane1

    def pull(values):
        return jnp.sum(jnp.where(hit, values, 0), axis=0, keepdims=True)

    source = pull(lax.broadcasted_iota(jnp.int32, (slots, 128), 0))
    upto = jnp.sum((row_col <= lane1).astype(jnp.int32), axis=0, keepdims=True)
    have = jnp.sum((row_col == lane1).astype(jnp.int32), axis=0, keepdims=True)
    for i, values in enumerate((pull(row_col), pull(col_col), jnp.maximum(upto - 1, 0), have, source >> 1, source & 1)):
        mall[0, i:i + 1] = values
    to_smem = [pltpu.make_async_copy(mall.at[i], smeta.at[i], loc.at[i]) for i in range(n_col)]
    to_smem[0].start()
    base = me_r * blocks
    for c in range(X_CHUNKS):
        for a, src in enumerate((coef, direc)):
            piece = src[:, c * part:(c + 1) * part].astype(jnp.float32).T.astype(jnp.bfloat16)
            xall[pl.ds(base + c * per, per), :, a * orbs:(a + 1) * orbs] = piece.reshape(per, BLOCK, orbs)
    lane = lax.broadcasted_iota(jnp.int32, (16, 2 * BLOCK), 1)

    def halves(flag):
        return [jnp.where((lane // BLOCK == h) & flag, 1.0, 0.0).astype(jnp.bfloat16)[None] for h in (0, 1)]

    to_smem[0].wait()
    for k in range(pairs):
        piece = None
        for h in (0, 1):
            held = tiles[smeta[0, 4, 2 * k + h]]
            turned = pltpu.roll(held.astype(jnp.float32), BLOCK, 1).astype(jnp.bfloat16)
            stays = smeta[0, 5, 2 * k + h] == h
            held, turned = (v.reshape(BLOCK // 16, 16, 2 * BLOCK) for v in (held, turned))
            part_of = held * halves(stays)[h] + turned * halves(jnp.logical_not(stays))[h]
            piece = part_of if piece is None else piece + part_of
        tall[0, k] = piece.reshape(BLOCK, 2 * BLOCK)
    pl.semaphore_wait(barrier, 2 + 1 + chips - 1)

    def x_ref(owner, c):
        return xall.at[pl.ds(owner * blocks + c * per, per)]

    def x_copy(owner, c, to, send, recv):
        return pltpu.make_async_remote_copy(
            src_ref=x_ref(owner, c), dst_ref=x_ref(owner, c), send_sem=send, recv_sem=recv,
            device_id=(to, me_c), device_id_type=MESH)

    def cross_to(k, c):
        return x_copy(me_r, c, ((chip + k) % chips) * 2 + core, cross_s.at[k - 1, c], cross_r.at[k - 1, c])

    def cross_from(k, c):
        owner = ((chip + chips - k) % chips) * 2 + core
        return x_copy(owner, c, owner, cross_s.at[k - 1, c], cross_r.at[k - 1, c])

    def sib_to(c):
        return x_copy(me_r, c, sibling, sib_s.at[c], sib_r.at[c])

    def sib_from(c):
        return x_copy(sibling, c, sibling, sib_s.at[c], sib_r.at[c])

    def fwd_to(k, c):
        owner = ((chip + chips - k) % chips) * 2 + core
        return x_copy(owner, c, sibling, fwd_s.at[k - 1, c], fwd_r.at[k - 1, c])

    def fwd_from(k, c):
        owner = ((chip + chips - k) % chips) * 2 + 1 - core
        return x_copy(owner, c, sibling, fwd_s.at[k - 1, c], fwd_r.at[k - 1, c])

    def ring_slots(d, t):
        return (t - 1, t) if d == 0 else ((n_col - t + 1) % n_col, n_col - t)

    def ring(d, t, h):
        a, b = ring_slots(d, t)
        cut = pl.ds(h * cut_pairs, cut_pairs)
        return pltpu.make_async_remote_copy(
            src_ref=tall.at[a, cut], dst_ref=tall.at[b, cut],
            send_sem=ring_s.at[d, t - 1, h], recv_sem=ring_r.at[d, t - 1, h],
            device_id=(me_r, nxt if d == 0 else prv), device_id_type=MESH)

    def meta(d, t):
        a, b = ring_slots(d, t)
        return pltpu.make_async_remote_copy(
            src_ref=mall.at[a], dst_ref=mall.at[b],
            send_sem=meta_s.at[d, t - 1], recv_sem=meta_r.at[d, t - 1],
            device_id=(me_r, nxt if d == 0 else prv), device_id_type=MESH)

    def ring_parts(t):
        if t < steps:
            return [(d, h) for h in range(HALVES) for d in (0, 1)], (0, 1)
        return [(0, 0), (1, 1)], (0,)

    def slot_of(q):
        return (q % 2) * ((q + 1) // 2) + (1 - q % 2) * ((n_col - q // 2) % n_col)

    def compute(q):
        slot = slot_of(q)
        carry = None
        for g in range(slots // 4):
            r = [smeta[slot, 0, 4 * g + i] for i in range(4)]
            blank = jnp.zeros((BLOCK, 2 * BLOCK), jnp.bfloat16)
            grid = []
            for a in range(4):
                line = []
                for u in range(2):
                    if a < 2 * u:
                        line.append(blank)
                        continue
                    lead = lane < BLOCK
                    keep = lead if a == 2 * u else jnp.where(lead, r[2 * u], r[2 * u + 1]) == r[a]
                    keep = jnp.where(keep, 1.0, 0.0).astype(jnp.bfloat16)
                    mats = tall[slot, 2 * g + u].reshape(BLOCK // 16, 16, 2 * BLOCK)
                    line.append((mats * keep[None]).reshape(BLOCK, 2 * BLOCK))
                grid.append(jnp.concatenate(line, axis=1))
            picked = jnp.concatenate([xall[smeta[slot, 1, 4 * g + i]] for i in range(4)], axis=0)
            got = jnp.dot(jnp.concatenate(grid, axis=0), picked, preferred_element_type=jnp.float32)
            for a in range(4):
                one = got[a * BLOCK:(a + 1) * BLOCK]
                if carry is not None:
                    one = one + jnp.where(r[a] == before, carry, 0.0)
                sums[4 * g + a] = one
            carry, before = one, r[3]
        for b in range(blocks):
            at = slice(b * BLOCK, (b + 1) * BLOCK)
            acc[at, :] += jnp.where(smeta[slot, 3, b] > 0, sums[smeta[slot, 2, b]], 0.0)

    def send_ring(t):
        pieces, metas = ring_parts(t)
        for d in metas:
            meta(d, t).start()
        for d, h in pieces:
            ring(d, t, h).start()

    def ring_event(t):
        pieces, metas = ring_parts(t)
        more, more_metas = ring_parts(t + 1) if t < steps else ((), ())
        for d in metas:
            meta(d, t).wait_recv()
            if d in more_metas:
                meta(d, t + 1).start()
        for d, h in pieces:
            ring(d, t, h).wait_recv()
            if (d, h) in more:
                ring(d, t + 1, h).start()
        for d in metas:
            to_smem[ring_slots(d, t)[1]].start()

    for c in range(X_CHUNKS):
        for k in range(1, chips):
            cross_to(k, c).start()
        if c == 0:
            send_ring(1)
    for c in range(X_CHUNKS):
        sib_to(c).start()
    acc[...] = jnp.zeros_like(acc)

    events = [(((k - 1) * X_CHUNKS + c + 1) * 2.6, 0, k, c) for k in range(1, chips) for c in range(X_CHUNKS)]
    events += [(t * 3.9, 1, t, 0) for t in range(1, steps)]
    for _, kind, k, c in sorted(events):
        if kind == 0:
            cross_from(k, c).wait_recv()
            fwd_to(k, c).start()
        else:
            ring_event(k)
    for c in range(X_CHUNKS):
        sib_from(c).wait_recv()
    for k in range(1, chips):
        for c in range(X_CHUNKS):
            fwd_from(k, c).wait_recv()

    for t in range(1, steps):
        for d in (0, 1):
            to_smem[ring_slots(d, t)[1]].wait()

    def shard(q, carry):
        compute(q)
        return carry

    lax.fori_loop(0, n_col - 1, shard, 0)
    ring_event(steps)
    to_smem[steps].wait()
    lax.fori_loop(n_col - 1, n_col, shard, 0)

    for a, out in enumerate((out_c, out_d)):
        for m in range(basis // 256):
            out[:, m * 256:(m + 1) * 256] = acc[m * 256:(m + 1) * 256, a * orbs:(a + 1) * orbs].T.astype(jnp.bfloat16)

    for c in range(X_CHUNKS):
        sib_to(c).wait_send()
        for k in range(1, chips):
            cross_to(k, c).wait_send()
            fwd_to(k, c).wait_send()
    for t in range(1, steps + 1):
        pieces, metas = ring_parts(t)
        for d in metas:
            meta(d, t).wait_send()
        for d, h in pieces:
            ring(d, t, h).wait_send()


def local(n_row, n_col, coefs, direction, tiles, block_rows, block_cols, counts):
    slots = tiles.shape[1]
    orbs, basis = coefs.shape
    width = 2 * orbs
    tile_mats = tiles[0].reshape(slots // 2, 2, BLOCK, BLOCK).transpose(0, 2, 1, 3).reshape(slots // 2, BLOCK, 2 * BLOCK)
    chips, steps = n_row // 2, n_col // 2
    vmem = pl.BlockSpec(memory_space=pltpu.VMEM)
    dma = pltpu.SemaphoreType.DMA
    out = jax.ShapeDtypeStruct((orbs, basis), jnp.bfloat16)
    return pl.pallas_call(
        functools.partial(kernel, n_row, n_col),
        out_shape=(out, out),
        in_specs=[vmem] * 5 + [pl.BlockSpec(memory_space=pltpu.SMEM)],
        out_specs=(vmem, vmem),
        scratch_shapes=[
            pltpu.VMEM((n_row * basis // BLOCK, BLOCK, width), jnp.bfloat16),
            pltpu.VMEM((n_col, slots // 2, BLOCK, 2 * BLOCK), jnp.bfloat16),
            pltpu.VMEM((n_col, 8, 128), jnp.int32),
            pltpu.SMEM((n_col, 8, 128), jnp.int32),
            pltpu.VMEM((slots, BLOCK, width), jnp.float32),
            pltpu.VMEM((basis, width), jnp.float32),
            dma((X_CHUNKS,)), dma((X_CHUNKS,)),
            dma((chips - 1, X_CHUNKS)), dma((chips - 1, X_CHUNKS)),
            dma((chips - 1, X_CHUNKS)), dma((chips - 1, X_CHUNKS)),
            dma((2, steps, HALVES)), dma((2, steps, HALVES)),
            dma((2, steps)), dma((2, steps)),
            dma((n_col,)),
        ],
        compiler_params=pltpu.CompilerParams(
            collective_id=0, has_side_effects=True, vmem_limit_bytes=56 * 2**20),
        name="block_sparse_apply",
    )(coefs, direction, tile_mats, block_rows, block_cols, counts)


def solution(mesh):
    body = functools.partial(local, mesh.shape["row"], mesh.shape["col"])
    return jax.shard_map(
        body,
        mesh=mesh,
        in_specs=(
            P("col", "row"),
            P("col", "row"),
            P("row", "col", None),
            P("row", "col"),
            P("row", "col"),
            P("row", "col"),
        ),
        out_specs=(P("col", "row"), P("col", "row")),
        check_vma=False,
    )
```

```python
import functools

import jax
import jax.numpy as jnp
from jax import lax
from jax.experimental import pallas as pl
from jax.experimental.pallas import tpu as pltpu
from jax.sharding import PartitionSpec as P

BLOCK = 64
X_CHUNKS = 4
HALVES = 2
MESH = pl.DeviceIdType.MESH


def kernel(n_row, n_col, coef, direc, tiles, rows, cols, counts, out_c, out_d,
           xall, tall, mall, smeta, sums, acc, flat, rows2,
           sib_s, sib_r, cross_s, cross_r, fwd_s, fwd_r, ring_s, ring_r, meta_s, meta_r, loc):
    orbs, basis = coef.shape
    width = 2 * orbs
    slots = rows.shape[1]
    blocks = basis // BLOCK
    pairs = slots // 2
    cut_pairs = pairs // HALVES
    chips = n_row // 2
    steps = n_col // 2
    part = basis // X_CHUNKS
    per = part // BLOCK

    me_r, me_c = lax.axis_index("row"), lax.axis_index("col")
    chip, core = me_r // 2, me_r % 2
    sibling = chip * 2 + 1 - core
    turn = me_c % 2
    pos = me_c // 2 + turn * (n_col - 1 - 2 * (me_c // 2))

    def at_pos(p):
        side = p // steps
        return 2 * (p + side * (n_col - 1 - 2 * p)) + side

    nxt, prv = at_pos((pos + 1) % n_col), at_pos((pos + n_col - 1) % n_col)

    barrier = pltpu.get_barrier_semaphore()
    for c in (nxt, prv):
        pl.semaphore_signal(barrier, inc=1, device_id=(me_r, c), device_id_type=MESH)
    pl.semaphore_signal(barrier, inc=1, device_id=(sibling, me_c), device_id_type=MESH)
    for k in range(1, chips):
        pl.semaphore_signal(barrier, inc=1, device_id=(((chip + k) % chips) * 2 + core, me_c), device_id_type=MESH)

    for m in range(BLOCK // 2):
        flat[:, m, :] = tiles[0, :, m * 2 * BLOCK:(m + 1) * 2 * BLOCK].astype(jnp.float32)

    lane1 = lax.broadcasted_iota(jnp.int32, (1, 128), 1)
    pad = lax.broadcasted_iota(jnp.int32, (8, 128), 0)
    row_key = jnp.where(lane1[:, :slots] < counts[0, 0], rows[...], blocks)
    mall[0] = jnp.zeros((8, 128), jnp.int32)
    mall[0, 0:1, 0:slots] = row_key * slots + lane1[:, :slots]
    mall[0, 1:2, 0:slots] = cols[...]
    mall[0, 2:3, 0:slots] = row_key
    wide = mall[0]
    tall_form = wide.T
    key_col, col_col, row_col = (tall_form[:slots, i:i + 1] for i in range(3))
    rank = jnp.sum((key_col < wide[0:1]).astype(jnp.int32), axis=0, keepdims=True)
    rank_col = jnp.where(pad == 0, rank, 0).T[:slots, 0:1]
    hit = rank_col == lane1

    def pull(values):
        return jnp.sum(jnp.where(hit, values, 0), axis=0, keepdims=True)

    source = pull(lax.broadcasted_iota(jnp.int32, (slots, 128), 0))
    upto = jnp.sum((row_col <= lane1).astype(jnp.int32), axis=0, keepdims=True)
    have = jnp.sum((row_col == lane1).astype(jnp.int32), axis=0, keepdims=True)
    for i, values in enumerate((pull(row_col), pull(col_col), jnp.maximum(upto - 1, 0), have, source)):
        mall[0, i:i + 1] = values
    to_smem = [pltpu.make_async_copy(mall.at[i], smeta.at[i], loc.at[i]) for i in range(n_col)]
    to_smem[0].start()
    base = me_r * blocks
    for c in range(X_CHUNKS):
        for a, src in enumerate((coef, direc)):
            piece = src[:, c * part:(c + 1) * part].astype(jnp.float32).T.astype(jnp.bfloat16)
            xall[pl.ds(base + c * per, per), :, a * orbs:(a + 1) * orbs] = piece.reshape(per, BLOCK, orbs)
    lane = lax.broadcasted_iota(jnp.int32, (16, 2 * BLOCK), 1)

    first = lax.broadcasted_iota(jnp.int32, (BLOCK // 2, 2 * BLOCK), 1) < BLOCK
    to_smem[0].wait()
    for k in range(pairs):
        one, two = flat[smeta[0, 4, 2 * k]], flat[smeta[0, 4, 2 * k + 1]]
        rows2[pl.ds(0, BLOCK // 2, stride=2), :] = jnp.where(first, one, pltpu.roll(two, BLOCK, 1))
        rows2[pl.ds(1, BLOCK // 2, stride=2), :] = jnp.where(first, pltpu.roll(one, BLOCK, 1), two)
        tall[0, k] = rows2[...].astype(jnp.bfloat16)
    pl.semaphore_wait(barrier, 2 + 1 + chips - 1)

    def x_ref(owner, c):
        return xall.at[pl.ds(owner * blocks + c * per, per)]

    def x_copy(owner, c, to, send, recv):
        return pltpu.make_async_remote_copy(
            src_ref=x_ref(owner, c), dst_ref=x_ref(owner, c), send_sem=send, recv_sem=recv,
            device_id=(to, me_c), device_id_type=MESH)

    def cross_to(k, c):
        return x_copy(me_r, c, ((chip + k) % chips) * 2 + core, cross_s.at[k - 1, c], cross_r.at[k - 1, c])

    def cross_from(k, c):
        owner = ((chip + chips - k) % chips) * 2 + core
        return x_copy(owner, c, owner, cross_s.at[k - 1, c], cross_r.at[k - 1, c])

    def sib_to(c):
        return x_copy(me_r, c, sibling, sib_s.at[c], sib_r.at[c])

    def sib_from(c):
        return x_copy(sibling, c, sibling, sib_s.at[c], sib_r.at[c])

    def fwd_to(k, c):
        owner = ((chip + chips - k) % chips) * 2 + core
        return x_copy(owner, c, sibling, fwd_s.at[k - 1, c], fwd_r.at[k - 1, c])

    def fwd_from(k, c):
        owner = ((chip + chips - k) % chips) * 2 + 1 - core
        return x_copy(owner, c, sibling, fwd_s.at[k - 1, c], fwd_r.at[k - 1, c])

    def ring_slots(d, t):
        return (t - 1, t) if d == 0 else ((n_col - t + 1) % n_col, n_col - t)

    def ring(d, t, h):
        a, b = ring_slots(d, t)
        cut = pl.ds(h * cut_pairs, cut_pairs)
        return pltpu.make_async_remote_copy(
            src_ref=tall.at[a, cut], dst_ref=tall.at[b, cut],
            send_sem=ring_s.at[d, t - 1, h], recv_sem=ring_r.at[d, t - 1, h],
            device_id=(me_r, nxt if d == 0 else prv), device_id_type=MESH)

    def meta(d, t):
        a, b = ring_slots(d, t)
        return pltpu.make_async_remote_copy(
            src_ref=mall.at[a], dst_ref=mall.at[b],
            send_sem=meta_s.at[d, t - 1], recv_sem=meta_r.at[d, t - 1],
            device_id=(me_r, nxt if d == 0 else prv), device_id_type=MESH)

    def ring_parts(t):
        if t < steps:
            return [(d, h) for h in range(HALVES) for d in (0, 1)], (0, 1)
        return [(0, 0), (1, 1)], (0,)

    def slot_of(q):
        return (q % 2) * ((q + 1) // 2) + (1 - q % 2) * ((n_col - q // 2) % n_col)

    def compute(q):
        slot = slot_of(q)
        carry = None
        for g in range(slots // 4):
            r = [smeta[slot, 0, 4 * g + i] for i in range(4)]
            blank = jnp.zeros((BLOCK, 2 * BLOCK), jnp.bfloat16)
            grid = []
            for a in range(4):
                line = []
                for u in range(2):
                    if a < 2 * u:
                        line.append(blank)
                        continue
                    lead = lane < BLOCK
                    keep = lead if a == 2 * u else jnp.where(lead, r[2 * u], r[2 * u + 1]) == r[a]
                    keep = jnp.where(keep, 1.0, 0.0).astype(jnp.bfloat16)
                    mats = tall[slot, 2 * g + u].reshape(BLOCK // 16, 16, 2 * BLOCK)
                    line.append((mats * keep[None]).reshape(BLOCK, 2 * BLOCK))
                grid.append(jnp.concatenate(line, axis=1))
            picked = jnp.concatenate([xall[smeta[slot, 1, 4 * g + i]] for i in range(4)], axis=0)
            got = jnp.dot(jnp.concatenate(grid, axis=0), picked, preferred_element_type=jnp.float32)
            for a in range(4):
                one = got[a * BLOCK:(a + 1) * BLOCK]
                if carry is not None:
                    one = one + jnp.where(r[a] == before, carry, 0.0)
                sums[4 * g + a] = one
            carry, before = one, r[3]
        for b in range(blocks):
            at = slice(b * BLOCK, (b + 1) * BLOCK)
            acc[at, :] += jnp.where(smeta[slot, 3, b] > 0, sums[smeta[slot, 2, b]], 0.0)

    def send_ring(t):
        pieces, metas = ring_parts(t)
        for d in metas:
            meta(d, t).start()
        for d, h in pieces:
            ring(d, t, h).start()

    def ring_event(t):
        pieces, metas = ring_parts(t)
        more, more_metas = ring_parts(t + 1) if t < steps else ((), ())
        for d in metas:
            meta(d, t).wait_recv()
            if d in more_metas:
                meta(d, t + 1).start()
        for d, h in pieces:
            ring(d, t, h).wait_recv()
            if (d, h) in more:
                ring(d, t + 1, h).start()
        for d in metas:
            to_smem[ring_slots(d, t)[1]].start()

    for c in range(X_CHUNKS):
        for k in range(1, chips):
            cross_to(k, c).start()
        if c == 0:
            send_ring(1)
    for c in range(X_CHUNKS):
        sib_to(c).start()
    acc[...] = jnp.zeros_like(acc)

    events = [(((k - 1) * X_CHUNKS + c + 1) * 2.6, 0, k, c) for k in range(1, chips) for c in range(X_CHUNKS)]
    events += [(t * 3.9, 1, t, 0) for t in range(1, steps)]
    for _, kind, k, c in sorted(events):
        if kind == 0:
            cross_from(k, c).wait_recv()
            fwd_to(k, c).start()
        else:
            ring_event(k)
    for c in range(X_CHUNKS):
        sib_from(c).wait_recv()
    for k in range(1, chips):
        for c in range(X_CHUNKS):
            fwd_from(k, c).wait_recv()

    for t in range(1, steps):
        for d in (0, 1):
            to_smem[ring_slots(d, t)[1]].wait()

    def shard(q, carry):
        compute(q)
        return carry

    lax.fori_loop(0, n_col - 1, shard, 0)
    ring_event(steps)
    to_smem[steps].wait()
    lax.fori_loop(n_col - 1, n_col, shard, 0)

    for a, out in enumerate((out_c, out_d)):
        for m in range(basis // 256):
            out[:, m * 256:(m + 1) * 256] = acc[m * 256:(m + 1) * 256, a * orbs:(a + 1) * orbs].T.astype(jnp.bfloat16)

    for c in range(X_CHUNKS):
        sib_to(c).wait_send()
        for k in range(1, chips):
            cross_to(k, c).wait_send()
            fwd_to(k, c).wait_send()
    for t in range(1, steps + 1):
        pieces, metas = ring_parts(t)
        for d in metas:
            meta(d, t).wait_send()
        for d, h in pieces:
            ring(d, t, h).wait_send()


def hand_over(a, b, out_a, out_b, sems):
    copies = [pltpu.make_async_copy(src, dst, sems.at[i]) for i, (src, dst) in enumerate(((a, out_a), (b, out_b)))]
    for copy in copies:
        copy.start()
    for copy in copies:
        copy.wait()


def local(n_row, n_col, coefs, direction, tiles, block_rows, block_cols, counts):
    slots = tiles.shape[1]
    orbs, basis = coefs.shape
    width = 2 * orbs
    chips, steps = n_row // 2, n_col // 2
    vmem = pl.BlockSpec(memory_space=pltpu.VMEM)
    dma = pltpu.SemaphoreType.DMA
    out = jax.ShapeDtypeStruct((orbs, basis), jnp.bfloat16)
    results = pl.pallas_call(
        functools.partial(kernel, n_row, n_col),
        out_shape=(out, out),
        in_specs=[vmem] * 5 + [pl.BlockSpec(memory_space=pltpu.SMEM)],
        out_specs=(vmem, vmem),
        scratch_shapes=[
            pltpu.VMEM((n_row * basis // BLOCK, BLOCK, width), jnp.bfloat16),
            pltpu.VMEM((n_col, slots // 2, BLOCK, 2 * BLOCK), jnp.bfloat16),
            pltpu.VMEM((n_col, 8, 128), jnp.int32),
            pltpu.SMEM((n_col, 8, 128), jnp.int32),
            pltpu.VMEM((slots, BLOCK, width), jnp.float32),
            pltpu.VMEM((basis, width), jnp.float32),
            pltpu.VMEM((slots, BLOCK // 2, 2 * BLOCK), jnp.float32),
            pltpu.VMEM((BLOCK, 2 * BLOCK), jnp.float32),
            dma((X_CHUNKS,)), dma((X_CHUNKS,)),
            dma((chips - 1, X_CHUNKS)), dma((chips - 1, X_CHUNKS)),
            dma((chips - 1, X_CHUNKS)), dma((chips - 1, X_CHUNKS)),
            dma((2, steps, HALVES)), dma((2, steps, HALVES)),
            dma((2, steps)), dma((2, steps)),
            dma((n_col,)),
        ],
        compiler_params=pltpu.CompilerParams(
            collective_id=0, has_side_effects=True, vmem_limit_bytes=56 * 2**20),
        name="block_sparse_apply",
    )(coefs, direction, tiles, block_rows, block_cols, counts)
    return tuple(pl.pallas_call(
        hand_over,
        out_shape=(out, out),
        in_specs=[pl.BlockSpec(memory_space=pl.ANY)] * 2,
        out_specs=(pl.BlockSpec(memory_space=pl.ANY),) * 2,
        scratch_shapes=[dma((2,))],
        name="hand_over",
    )(*results))


def solution(mesh):
    body = functools.partial(local, mesh.shape["row"], mesh.shape["col"])
    return jax.shard_map(
        body,
        mesh=mesh,
        in_specs=(
            P("col", "row"),
            P("col", "row"),
            P("row", "col", None),
            P("row", "col"),
            P("row", "col"),
            P("row", "col"),
        ),
        out_specs=(P("col", "row"), P("col", "row")),
        check_vma=False,
    )
```

```python
import functools

import jax
import jax.numpy as jnp
from jax import lax
from jax.experimental import pallas as pl
from jax.experimental.pallas import tpu as pltpu
from jax.sharding import PartitionSpec as P

BLOCK = 64
X_CHUNKS = 2
HALVES = 2
MESH = pl.DeviceIdType.MESH


def kernel(n_row, n_col, coef, direc, tiles, rows, cols, counts, out_c, out_d,
           xall, tall, mall, smeta, sums, acc, flat, rows2,
           sib_s, sib_r, cross_s, cross_r, fwd_s, fwd_r, ring_s, ring_r, meta_s, meta_r, loc):
    orbs, basis = coef.shape
    width = 2 * orbs
    slots = rows.shape[1]
    blocks = basis // BLOCK
    pairs = slots // 2
    cut_pairs = pairs // HALVES
    chips = n_row // 2
    steps = n_col // 2
    part = basis // X_CHUNKS
    per = part // BLOCK
    x_parts = [(a, c) for a in (0, 1) for c in range(X_CHUNKS)]

    me_r, me_c = lax.axis_index("row"), lax.axis_index("col")
    chip, core = me_r // 2, me_r % 2
    sibling = chip * 2 + 1 - core
    turn = me_c % 2
    pos = me_c // 2 + turn * (n_col - 1 - 2 * (me_c // 2))

    def at_pos(p):
        side = p // steps
        return 2 * (p + side * (n_col - 1 - 2 * p)) + side

    nxt, prv = at_pos((pos + 1) % n_col), at_pos((pos + n_col - 1) % n_col)

    barrier = pltpu.get_barrier_semaphore()
    for c in (nxt, prv):
        pl.semaphore_signal(barrier, inc=1, device_id=(me_r, c), device_id_type=MESH)
    pl.semaphore_signal(barrier, inc=1, device_id=(sibling, me_c), device_id_type=MESH)
    for k in range(1, chips):
        pl.semaphore_signal(barrier, inc=1, device_id=(((chip + k) % chips) * 2 + core, me_c), device_id_type=MESH)

    lane1 = lax.broadcasted_iota(jnp.int32, (1, 128), 1)
    pad = lax.broadcasted_iota(jnp.int32, (8, 128), 0)
    row_key = jnp.where(lane1[:, :slots] < counts[0, 0], rows[...], blocks)
    mall[0] = jnp.zeros((8, 128), jnp.int32)
    mall[0, 0:1, 0:slots] = row_key * slots + lane1[:, :slots]
    mall[0, 1:2, 0:slots] = cols[...]
    mall[0, 2:3, 0:slots] = row_key
    wide = mall[0]
    tall_form = wide.T
    key_col, col_col, row_col = (tall_form[:slots, i:i + 1] for i in range(3))
    rank = jnp.sum((key_col < wide[0:1]).astype(jnp.int32), axis=0, keepdims=True)
    moves = jnp.where(rank[:, :slots] == lax.broadcasted_iota(jnp.int32, (slots, slots), 0), 1.0, 0.0)
    in_order = jnp.dot(moves.astype(jnp.bfloat16), tiles[0], preferred_element_type=jnp.float32)
    for m in range(BLOCK // 2):
        flat[:, m, :] = in_order[:, m * 2 * BLOCK:(m + 1) * 2 * BLOCK]
    first = lax.broadcasted_iota(jnp.int32, (BLOCK // 2, 2 * BLOCK), 1) < BLOCK
    for k in range(pairs):
        one, two = flat[2 * k], flat[2 * k + 1]
        rows2[k, pl.ds(0, BLOCK // 2, stride=2), :] = jnp.where(first, one, pltpu.roll(two, BLOCK, 1))
        rows2[k, pl.ds(1, BLOCK // 2, stride=2), :] = jnp.where(first, pltpu.roll(one, BLOCK, 1), two)
        tall[0, k] = rows2[k].astype(jnp.bfloat16)
    rank_col = jnp.where(pad == 0, rank, 0).T[:slots, 0:1]
    hit = rank_col == lane1

    def pull(values):
        return jnp.sum(jnp.where(hit, values, 0), axis=0, keepdims=True)

    upto = jnp.sum((row_col <= lane1).astype(jnp.int32), axis=0, keepdims=True)
    have = jnp.sum((row_col == lane1).astype(jnp.int32), axis=0, keepdims=True)
    for i, values in enumerate((pull(row_col), pull(col_col), jnp.maximum(upto - 1, 0), have)):
        mall[0, i:i + 1] = values
    to_smem = [pltpu.make_async_copy(mall.at[i], smeta.at[i], loc.at[i]) for i in range(n_col)]
    lane = lax.broadcasted_iota(jnp.int32, (16, 2 * BLOCK), 1)
    base = me_r * blocks
    pl.semaphore_wait(barrier, 2 + 1 + chips - 1)

    def x_ref(owner, c):
        return xall.at[c // X_CHUNKS, pl.ds(owner * blocks + c % X_CHUNKS * per, per)]

    def x_copy(owner, c, to, send, recv):
        return pltpu.make_async_remote_copy(
            src_ref=x_ref(owner, c), dst_ref=x_ref(owner, c), send_sem=send, recv_sem=recv,
            device_id=(to, me_c), device_id_type=MESH)

    def cross_to(k, c):
        return x_copy(me_r, c, ((chip + k) % chips) * 2 + core, cross_s.at[k - 1, c], cross_r.at[k - 1, c])

    def cross_from(k, c):
        owner = ((chip + chips - k) % chips) * 2 + core
        return x_copy(owner, c, owner, cross_s.at[k - 1, c], cross_r.at[k - 1, c])

    def sib_to(c):
        return x_copy(me_r, c, sibling, sib_s.at[c], sib_r.at[c])

    def sib_from(c):
        return x_copy(sibling, c, sibling, sib_s.at[c], sib_r.at[c])

    def fwd_to(k, c):
        owner = ((chip + chips - k) % chips) * 2 + core
        return x_copy(owner, c, sibling, fwd_s.at[k - 1, c], fwd_r.at[k - 1, c])

    def fwd_from(k, c):
        owner = ((chip + chips - k) % chips) * 2 + 1 - core
        return x_copy(owner, c, sibling, fwd_s.at[k - 1, c], fwd_r.at[k - 1, c])

    def ring_slots(d, t):
        return (t - 1, t) if d == 0 else ((n_col - t + 1) % n_col, n_col - t)

    def ring(d, t, h):
        a, b = ring_slots(d, t)
        cut = pl.ds(h * cut_pairs, cut_pairs)
        return pltpu.make_async_remote_copy(
            src_ref=tall.at[a, cut], dst_ref=tall.at[b, cut],
            send_sem=ring_s.at[d, t - 1, h], recv_sem=ring_r.at[d, t - 1, h],
            device_id=(me_r, nxt if d == 0 else prv), device_id_type=MESH)

    def meta(d, t):
        a, b = ring_slots(d, t)
        return pltpu.make_async_remote_copy(
            src_ref=mall.at[a], dst_ref=mall.at[b],
            send_sem=meta_s.at[d, t - 1], recv_sem=meta_r.at[d, t - 1],
            device_id=(me_r, nxt if d == 0 else prv), device_id_type=MESH)

    def ring_parts(t):
        if t < steps:
            return [(d, h) for h in range(HALVES) for d in (0, 1)], (0, 1)
        return [(0, 0), (1, 1)], (0,)

    def slot_of(q):
        return (q % 2) * ((q + 1) // 2) + (1 - q % 2) * ((n_col - q // 2) % n_col)

    def compute(q):
        slot = slot_of(q)
        carry = None
        for g in range(slots // 4):
            r = [smeta[slot, 0, 4 * g + i] for i in range(4)]
            blank = jnp.zeros((BLOCK, 2 * BLOCK), jnp.bfloat16)
            grid = []
            for a in range(4):
                line = []
                for u in range(2):
                    if a < 2 * u:
                        line.append(blank)
                        continue
                    lead = lane < BLOCK
                    keep = lead if a == 2 * u else jnp.where(lead, r[2 * u], r[2 * u + 1]) == r[a]
                    keep = jnp.where(keep, 1.0, 0.0).astype(jnp.bfloat16)
                    mats = tall[slot, 2 * g + u].reshape(BLOCK // 16, 16, 2 * BLOCK)
                    line.append((mats * keep[None]).reshape(BLOCK, 2 * BLOCK))
                grid.append(jnp.concatenate(line, axis=1))
            where = [smeta[slot, 1, 4 * g + i] for i in range(4)]
            picked = jnp.concatenate([
                jnp.concatenate([xall[a, c] for c in where], axis=0) for a in (0, 1)], axis=1)
            got = jnp.dot(jnp.concatenate(grid, axis=0), picked, preferred_element_type=jnp.float32)
            for a in range(4):
                one = got[a * BLOCK:(a + 1) * BLOCK]
                if carry is not None:
                    one = one + jnp.where(r[a] == before, carry, 0.0)
                sums[q * slots + 4 * g + a] = one
            carry, before = one, r[3]

    def add_rows(qs, begin):
        def row(b, carry):
            total = None if begin else acc[b]
            for q in qs:
                slot = slot_of(q)
                one = jnp.where(smeta[slot, 3, b] > 0, sums[q * slots + smeta[slot, 2, b]], 0.0)
                total = one if total is None else total + one
            acc[b] = total
            return carry

        lax.fori_loop(0, blocks, row, 0, unroll=4)

    def send_ring(t):
        pieces, metas = ring_parts(t)
        for d in metas:
            meta(d, t).start()
        for d, h in pieces:
            ring(d, t, h).start()

    def ring_event(t):
        pieces, metas = ring_parts(t)
        more, more_metas = ring_parts(t + 1) if t < steps else ((), ())
        for d in metas:
            meta(d, t).wait_recv()
            if d in more_metas:
                meta(d, t + 1).start()
        for d, h in pieces:
            ring(d, t, h).wait_recv()
            if (d, h) in more:
                ring(d, t + 1, h).start()
        for d in metas:
            to_smem[ring_slots(d, t)[1]].start()

    send_ring(1)
    for i, (a, c) in enumerate(x_parts):
        piece = (coef, direc)[a][:, c * part:(c + 1) * part].astype(jnp.float32).T.astype(jnp.bfloat16)
        xall[a, pl.ds(base + c * per, per)] = piece.reshape(per, BLOCK, orbs)
        for k in range(1, chips):
            cross_to(k, i).start()
        sib_to(i).start()
    to_smem[0].start()
    to_smem[0].wait()

    events = [(((k - 1) * len(x_parts) + c + 1) * 2.6, 0, k, c) for k in range(1, chips) for c in range(len(x_parts))]
    events += [(t * 3.9, 1, t, 0) for t in range(1, steps)]
    for _, kind, k, c in sorted(events):
        if kind == 0:
            cross_from(k, c).wait_recv()
            fwd_to(k, c).start()
        else:
            ring_event(k)
    for c in range(len(x_parts)):
        sib_from(c).wait_recv()
    for k in range(1, chips):
        for c in range(len(x_parts)):
            fwd_from(k, c).wait_recv()

    for t in range(1, steps):
        for d in (0, 1):
            to_smem[ring_slots(d, t)[1]].wait()

    def shard(q, carry):
        compute(q)
        return carry

    lax.fori_loop(0, n_col - 1, shard, 0)
    add_rows(range(n_col - 1), True)
    ring_event(steps)
    to_smem[steps].wait()
    lax.fori_loop(n_col - 1, n_col, shard, 0)
    add_rows((n_col - 1,), False)

    for a, out in enumerate((out_c, out_d)):
        for m in range(basis // 256):
            out[:, m * 256:(m + 1) * 256] = acc[4 * m:4 * m + 4, :, a * orbs:(a + 1) * orbs].reshape(256, orbs).T.astype(jnp.bfloat16)

    for c in range(len(x_parts)):
        sib_to(c).wait_send()
        for k in range(1, chips):
            cross_to(k, c).wait_send()
            fwd_to(k, c).wait_send()
    for t in range(1, steps + 1):
        pieces, metas = ring_parts(t)
        for d in metas:
            meta(d, t).wait_send()
        for d, h in pieces:
            ring(d, t, h).wait_send()


def hand_over(a, b, out_a, out_b):
    out_a[...] = a[...]
    out_b[...] = b[...]


def local(n_row, n_col, coefs, direction, tiles, block_rows, block_cols, counts):
    slots = tiles.shape[1]
    orbs, basis = coefs.shape
    width = 2 * orbs
    chips, steps = n_row // 2, n_col // 2
    vmem = pl.BlockSpec(memory_space=pltpu.VMEM)
    dma = pltpu.SemaphoreType.DMA
    out = jax.ShapeDtypeStruct((orbs, basis), jnp.bfloat16)
    results = pl.pallas_call(
        functools.partial(kernel, n_row, n_col),
        out_shape=(out, out),
        in_specs=[vmem] * 5 + [pl.BlockSpec(memory_space=pltpu.SMEM)],
        out_specs=(vmem, vmem),
        scratch_shapes=[
            pltpu.VMEM((2, n_row * basis // BLOCK, BLOCK, orbs), jnp.bfloat16),
            pltpu.VMEM((n_col, slots // 2, BLOCK, 2 * BLOCK), jnp.bfloat16),
            pltpu.VMEM((n_col, 8, 128), jnp.int32),
            pltpu.SMEM((n_col, 8, 128), jnp.int32),
            pltpu.VMEM((n_col * slots, BLOCK, width), jnp.float32),
            pltpu.VMEM((basis // BLOCK, BLOCK, width), jnp.float32),
            pltpu.VMEM((slots, BLOCK // 2, 2 * BLOCK), jnp.float32),
            pltpu.VMEM((slots // 2, BLOCK, 2 * BLOCK), jnp.float32),
            dma((2 * X_CHUNKS,)), dma((2 * X_CHUNKS,)),
            dma((chips - 1, 2 * X_CHUNKS)), dma((chips - 1, 2 * X_CHUNKS)),
            dma((chips - 1, 2 * X_CHUNKS)), dma((chips - 1, 2 * X_CHUNKS)),
            dma((2, steps, HALVES)), dma((2, steps, HALVES)),
            dma((2, steps)), dma((2, steps)),
            dma((n_col,)),
        ],
        compiler_params=pltpu.CompilerParams(
            collective_id=0, has_side_effects=True, vmem_limit_bytes=56 * 2**20),
        name="block_sparse_apply",
    )(coefs, direction, tiles, block_rows, block_cols, counts)
    return tuple(pl.pallas_call(
        hand_over,
        out_shape=(out, out),
        in_specs=[vmem] * 2,
        out_specs=(vmem, vmem),
        name="hand_over",
    )(*results))


def solution(mesh):
    body = functools.partial(local, mesh.shape["row"], mesh.shape["col"])
    return jax.shard_map(
        body,
        mesh=mesh,
        in_specs=(
            P("col", "row"),
            P("col", "row"),
            P("row", "col", None),
            P("row", "col"),
            P("row", "col"),
            P("row", "col"),
        ),
        out_specs=(P("col", "row"), P("col", "row")),
        check_vma=False,
    )
```

```python
import functools

import jax
import jax.numpy as jnp
from jax import lax
from jax.experimental import pallas as pl
from jax.experimental.pallas import tpu as pltpu
from jax.sharding import PartitionSpec as P

BLOCK = 64
X_CHUNKS = 2
HALVES = 2
MESH = pl.DeviceIdType.MESH


def kernel(n_row, n_col, coef, direc, tiles, rows, cols, counts, out_c, out_d,
           x_coef, x_direc, tall, mall, smeta, sums, acc, flat, rows2,
           sib_s, sib_r, cross_s, cross_r, fwd_s, fwd_r, ring_s, ring_r, meta_s, meta_r, loc):
    orbs, basis = coef.shape
    width = 2 * orbs
    slots = rows.shape[1]
    blocks = basis // BLOCK
    pairs = slots // 2
    cut_pairs = pairs // HALVES
    chips = n_row // 2
    steps = n_col // 2
    part = basis // X_CHUNKS
    per = part // BLOCK
    xall = (x_coef, x_direc)
    x_parts = [(a, c) for a in (0, 1) for c in range(X_CHUNKS)]

    me_r, me_c = lax.axis_index("row"), lax.axis_index("col")
    chip, core = me_r // 2, me_r % 2
    sibling = chip * 2 + 1 - core
    turn = me_c % 2
    pos = me_c // 2 + turn * (n_col - 1 - 2 * (me_c // 2))

    def at_pos(p):
        side = p // steps
        return 2 * (p + side * (n_col - 1 - 2 * p)) + side

    nxt, prv = at_pos((pos + 1) % n_col), at_pos((pos + n_col - 1) % n_col)

    barrier = pltpu.get_barrier_semaphore()
    for c in (nxt, prv):
        pl.semaphore_signal(barrier, inc=1, device_id=(me_r, c), device_id_type=MESH)
    pl.semaphore_signal(barrier, inc=1, device_id=(sibling, me_c), device_id_type=MESH)
    for k in range(1, chips):
        pl.semaphore_signal(barrier, inc=1, device_id=(((chip + k) % chips) * 2 + core, me_c), device_id_type=MESH)

    lane1 = lax.broadcasted_iota(jnp.int32, (1, 128), 1)
    pad = lax.broadcasted_iota(jnp.int32, (8, 128), 0)
    row_key = jnp.where(lane1[:, :slots] < counts[0, 0], rows[...], blocks)
    mall[0] = jnp.zeros((8, 128), jnp.int32)
    mall[0, 0:1, 0:slots] = row_key * slots + lane1[:, :slots]
    mall[0, 1:2, 0:slots] = cols[...]
    mall[0, 2:3, 0:slots] = row_key
    wide = mall[0]
    tall_form = wide.T
    key_col, col_col, row_col = (tall_form[:slots, i:i + 1] for i in range(3))
    rank = jnp.sum((key_col < wide[0:1]).astype(jnp.int32), axis=0, keepdims=True)
    moves = jnp.where(rank[:, :slots] == lax.broadcasted_iota(jnp.int32, (slots, slots), 0), 1.0, 0.0)
    in_order = jnp.dot(moves.astype(jnp.bfloat16), tiles[0], preferred_element_type=jnp.float32)
    for m in range(BLOCK // 2):
        flat[:, m, :] = in_order[:, m * 2 * BLOCK:(m + 1) * 2 * BLOCK]
    first = lax.broadcasted_iota(jnp.int32, (BLOCK // 2, 2 * BLOCK), 1) < BLOCK
    for k in range(pairs):
        one, two = flat[2 * k], flat[2 * k + 1]
        rows2[k, pl.ds(0, BLOCK // 2, stride=2), :] = jnp.where(first, one, pltpu.roll(two, BLOCK, 1))
        rows2[k, pl.ds(1, BLOCK // 2, stride=2), :] = jnp.where(first, pltpu.roll(one, BLOCK, 1), two)
        tall[0, k] = rows2[k].astype(jnp.bfloat16)
    rank_col = jnp.where(pad == 0, rank, 0).T[:slots, 0:1]
    hit = rank_col == lane1

    def pull(values):
        return jnp.sum(jnp.where(hit, values, 0), axis=0, keepdims=True)

    upto = jnp.sum((row_col <= lane1).astype(jnp.int32), axis=0, keepdims=True)
    have = jnp.sum((row_col == lane1).astype(jnp.int32), axis=0, keepdims=True)
    for i, values in enumerate((pull(row_col), pull(col_col), jnp.maximum(upto - 1, 0), have)):
        mall[0, i:i + 1] = values
    to_smem = [pltpu.make_async_copy(mall.at[i], smeta.at[i], loc.at[i]) for i in range(n_col)]
    lane = lax.broadcasted_iota(jnp.int32, (16, 2 * BLOCK), 1)
    base = me_r * blocks
    pl.semaphore_wait(barrier, 2 + 1 + chips - 1)

    def x_ref(owner, c):
        return xall[c // X_CHUNKS].at[pl.ds(owner * blocks + c % X_CHUNKS * per, per)]

    def x_copy(owner, c, to, send, recv):
        return pltpu.make_async_remote_copy(
            src_ref=x_ref(owner, c), dst_ref=x_ref(owner, c), send_sem=send, recv_sem=recv,
            device_id=(to, me_c), device_id_type=MESH)

    def cross_to(k, c):
        return x_copy(me_r, c, ((chip + k) % chips) * 2 + core, cross_s.at[k - 1, c], cross_r.at[k - 1, c])

    def cross_from(k, c):
        owner = ((chip + chips - k) % chips) * 2 + core
        return x_copy(owner, c, owner, cross_s.at[k - 1, c], cross_r.at[k - 1, c])

    def sib_to(c):
        return x_copy(me_r, c, sibling, sib_s.at[c], sib_r.at[c])

    def sib_from(c):
        return x_copy(sibling, c, sibling, sib_s.at[c], sib_r.at[c])

    def fwd_to(k, c):
        owner = ((chip + chips - k) % chips) * 2 + core
        return x_copy(owner, c, sibling, fwd_s.at[k - 1, c], fwd_r.at[k - 1, c])

    def fwd_from(k, c):
        owner = ((chip + chips - k) % chips) * 2 + 1 - core
        return x_copy(owner, c, sibling, fwd_s.at[k - 1, c], fwd_r.at[k - 1, c])

    def ring_slots(d, t):
        return (t - 1, t) if d == 0 else ((n_col - t + 1) % n_col, n_col - t)

    def ring(d, t, h):
        a, b = ring_slots(d, t)
        cut = pl.ds(h * cut_pairs, cut_pairs)
        return pltpu.make_async_remote_copy(
            src_ref=tall.at[a, cut], dst_ref=tall.at[b, cut],
            send_sem=ring_s.at[d, t - 1, h], recv_sem=ring_r.at[d, t - 1, h],
            device_id=(me_r, nxt if d == 0 else prv), device_id_type=MESH)

    def meta(d, t):
        a, b = ring_slots(d, t)
        return pltpu.make_async_remote_copy(
            src_ref=mall.at[a], dst_ref=mall.at[b],
            send_sem=meta_s.at[d, t - 1], recv_sem=meta_r.at[d, t - 1],
            device_id=(me_r, nxt if d == 0 else prv), device_id_type=MESH)

    def ring_parts(t):
        if t < steps:
            return [(d, h) for h in range(HALVES) for d in (0, 1)], (0, 1)
        return [(0, 0), (1, 1)], (0,)

    def slot_of(q):
        return (q % 2) * ((q + 1) // 2) + (1 - q % 2) * ((n_col - q // 2) % n_col)

    def compute(q, arrays):
        lanes = slice(arrays[0] * orbs, (arrays[-1] + 1) * orbs)
        slot = slot_of(q)
        carry = None
        for g in range(slots // 4):
            r = [smeta[slot, 0, 4 * g + i] for i in range(4)]
            blank = jnp.zeros((BLOCK, 2 * BLOCK), jnp.bfloat16)
            grid = []
            for a in range(4):
                line = []
                for u in range(2):
                    if a < 2 * u:
                        line.append(blank)
                        continue
                    lead = lane < BLOCK
                    keep = lead if a == 2 * u else jnp.where(lead, r[2 * u], r[2 * u + 1]) == r[a]
                    keep = jnp.where(keep, 1.0, 0.0).astype(jnp.bfloat16)
                    mats = tall[slot, 2 * g + u].reshape(BLOCK // 16, 16, 2 * BLOCK)
                    line.append((mats * keep[None]).reshape(BLOCK, 2 * BLOCK))
                grid.append(jnp.concatenate(line, axis=1))
            where = [smeta[slot, 1, 4 * g + i] for i in range(4)]
            picked = jnp.concatenate([
                jnp.concatenate([xall[a][c] for c in where], axis=0) for a in arrays], axis=1)
            got = jnp.dot(jnp.concatenate(grid, axis=0), picked, preferred_element_type=jnp.float32)
            for a in range(4):
                one = got[a * BLOCK:(a + 1) * BLOCK]
                if carry is not None:
                    one = one + jnp.where(r[a] == before, carry, 0.0)
                sums[q * slots + 4 * g + a, :, lanes] = one
            carry, before = one, r[3]

    def add_rows(qs, begin):
        def row(b, carry):
            total = None if begin else acc[b]
            for q in qs:
                slot = slot_of(q)
                one = jnp.where(smeta[slot, 3, b] > 0, sums[q * slots + smeta[slot, 2, b]], 0.0)
                total = one if total is None else total + one
            acc[b] = total
            return carry

        lax.fori_loop(0, blocks, row, 0, unroll=4)

    def send_ring(t):
        pieces, metas = ring_parts(t)
        for d in metas:
            meta(d, t).start()
        for d, h in pieces:
            ring(d, t, h).start()

    def ring_event(t):
        pieces, metas = ring_parts(t)
        more, more_metas = ring_parts(t + 1) if t < steps else ((), ())
        for d in metas:
            meta(d, t).wait_recv()
            if d in more_metas:
                meta(d, t + 1).start()
        for d, h in pieces:
            ring(d, t, h).wait_recv()
            if (d, h) in more:
                ring(d, t + 1, h).start()
        for d in metas:
            to_smem[ring_slots(d, t)[1]].start()

    send_ring(1)
    for i, (a, c) in enumerate(x_parts):
        piece = (coef, direc)[a][:, c * part:(c + 1) * part].astype(jnp.float32).T.astype(jnp.bfloat16)
        xall[a][pl.ds(base + c * per, per)] = piece.reshape(per, BLOCK, orbs)
        for k in range(1, chips):
            cross_to(k, i).start()
        sib_to(i).start()
    to_smem[0].start()
    to_smem[0].wait()

    def shards(begin, end, arrays):
        def shard(q, carry):
            compute(q, arrays)
            return carry

        lax.fori_loop(begin, end, shard, 0)

    def cross_events(a):
        for i in range(a * X_CHUNKS, (a + 1) * X_CHUNKS):
            for k in range(1, chips):
                cross_from(k, i).wait_recv()
                fwd_to(k, i).start()

    def settle(a):
        for i in range(a * X_CHUNKS, (a + 1) * X_CHUNKS):
            sib_from(i).wait_recv()
            for k in range(1, chips):
                fwd_from(k, i).wait_recv()

    def list_here(t):
        for d in (0, 1):
            to_smem[ring_slots(d, t)[1]].wait()

    ring_event(1)
    cross_events(0)
    settle(0)
    list_here(1)
    shards(0, 3, (0,))
    ring_event(2)
    list_here(2)
    shards(3, 5, (0,))
    cross_events(1)
    for t in range(3, steps):
        ring_event(t)
    settle(1)
    shards(0, 5, (1,))
    for t in range(3, steps):
        list_here(t)
    shards(5, n_col - 1, (0, 1))
    add_rows(range(n_col - 1), True)
    ring_event(steps)
    to_smem[steps].wait()
    shards(n_col - 1, n_col, (0, 1))
    add_rows((n_col - 1,), False)

    for a, out in enumerate((out_c, out_d)):
        for m in range(basis // 256):
            out[:, m * 256:(m + 1) * 256] = acc[4 * m:4 * m + 4, :, a * orbs:(a + 1) * orbs].reshape(256, orbs).T.astype(jnp.bfloat16)

    for c in range(len(x_parts)):
        sib_to(c).wait_send()
        for k in range(1, chips):
            cross_to(k, c).wait_send()
            fwd_to(k, c).wait_send()
    for t in range(1, steps + 1):
        pieces, metas = ring_parts(t)
        for d in metas:
            meta(d, t).wait_send()
        for d, h in pieces:
            ring(d, t, h).wait_send()


def hand_over(a, b, out_a, out_b):
    out_a[...] = a[...]
    out_b[...] = b[...]


def local(n_row, n_col, coefs, direction, tiles, block_rows, block_cols, counts):
    slots = tiles.shape[1]
    orbs, basis = coefs.shape
    width = 2 * orbs
    chips, steps = n_row // 2, n_col // 2
    vmem = pl.BlockSpec(memory_space=pltpu.VMEM)
    dma = pltpu.SemaphoreType.DMA
    out = jax.ShapeDtypeStruct((orbs, basis), jnp.bfloat16)
    results = pl.pallas_call(
        functools.partial(kernel, n_row, n_col),
        out_shape=(out, out),
        in_specs=[vmem] * 5 + [pl.BlockSpec(memory_space=pltpu.SMEM)],
        out_specs=(vmem, vmem),
        scratch_shapes=[
            pltpu.VMEM((n_row * basis // BLOCK, BLOCK, orbs), jnp.bfloat16),
            pltpu.VMEM((n_row * basis // BLOCK, BLOCK, orbs), jnp.bfloat16),
            pltpu.VMEM((n_col, slots // 2, BLOCK, 2 * BLOCK), jnp.bfloat16),
            pltpu.VMEM((n_col, 8, 128), jnp.int32),
            pltpu.SMEM((n_col, 8, 128), jnp.int32),
            pltpu.VMEM((n_col * slots, BLOCK, width), jnp.float32),
            pltpu.VMEM((basis // BLOCK, BLOCK, width), jnp.float32),
            pltpu.VMEM((slots, BLOCK // 2, 2 * BLOCK), jnp.float32),
            pltpu.VMEM((slots // 2, BLOCK, 2 * BLOCK), jnp.float32),
            dma((2 * X_CHUNKS,)), dma((2 * X_CHUNKS,)),
            dma((chips - 1, 2 * X_CHUNKS)), dma((chips - 1, 2 * X_CHUNKS)),
            dma((chips - 1, 2 * X_CHUNKS)), dma((chips - 1, 2 * X_CHUNKS)),
            dma((2, steps, HALVES)), dma((2, steps, HALVES)),
            dma((2, steps)), dma((2, steps)),
            dma((n_col,)),
        ],
        compiler_params=pltpu.CompilerParams(
            collective_id=0, has_side_effects=True, vmem_limit_bytes=56 * 2**20),
        name="block_sparse_apply",
    )(coefs, direction, tiles, block_rows, block_cols, counts)
    return tuple(pl.pallas_call(
        hand_over,
        out_shape=(out, out),
        in_specs=[vmem] * 2,
        out_specs=(vmem, vmem),
        name="hand_over",
    )(*results))


def solution(mesh):
    body = functools.partial(local, mesh.shape["row"], mesh.shape["col"])
    return jax.shard_map(
        body,
        mesh=mesh,
        in_specs=(
            P("col", "row"),
            P("col", "row"),
            P("row", "col", None),
            P("row", "col"),
            P("row", "col"),
            P("row", "col"),
        ),
        out_specs=(P("col", "row"), P("col", "row")),
        check_vma=False,
    )
```

```python
import functools

import jax
import jax.numpy as jnp
from jax import lax
from jax.experimental import pallas as pl
from jax.experimental.pallas import tpu as pltpu
from jax.sharding import PartitionSpec as P

BLOCK = 64
X_CHUNKS = 2
HALVES = 2
MESH = pl.DeviceIdType.MESH


def kernel(n_row, n_col, coef, direc, tiles, rows, cols, counts, out_c, out_d,
           x_coef, x_direc, tall, mall, smeta, sums, acc, flat, rows2,
           sib_s, sib_r, cross_s, cross_r, fwd_s, fwd_r, ring_s, ring_r, meta_s, meta_r, loc):
    orbs, basis = coef.shape
    width = 2 * orbs
    slots = rows.shape[1]
    blocks = basis // BLOCK
    pairs = slots // 2
    cut_pairs = pairs // HALVES
    chips = n_row // 2
    steps = n_col // 2
    part = basis // X_CHUNKS
    per = part // BLOCK
    xall = (x_coef, x_direc)
    x_parts = [(a, c) for a in (0, 1) for c in range(X_CHUNKS)]

    me_r, me_c = lax.axis_index("row"), lax.axis_index("col")
    chip, core = me_r // 2, me_r % 2
    sibling = chip * 2 + 1 - core
    turn = me_c % 2
    pos = me_c // 2 + turn * (n_col - 1 - 2 * (me_c // 2))

    def at_pos(p):
        side = p // steps
        return 2 * (p + side * (n_col - 1 - 2 * p)) + side

    nxt, prv = at_pos((pos + 1) % n_col), at_pos((pos + n_col - 1) % n_col)

    barrier = pltpu.get_barrier_semaphore()
    for c in (nxt, prv):
        pl.semaphore_signal(barrier, inc=1, device_id=(me_r, c), device_id_type=MESH)
    pl.semaphore_signal(barrier, inc=1, device_id=(sibling, me_c), device_id_type=MESH)
    for k in range(1, chips):
        pl.semaphore_signal(barrier, inc=1, device_id=(((chip + k) % chips) * 2 + core, me_c), device_id_type=MESH)

    lane1 = lax.broadcasted_iota(jnp.int32, (1, 128), 1)
    pad = lax.broadcasted_iota(jnp.int32, (8, 128), 0)
    row_key = jnp.where(lane1[:, :slots] < counts[0, 0], rows[...], blocks)
    mall[0] = jnp.zeros((8, 128), jnp.int32)
    mall[0, 0:1, 0:slots] = row_key * slots + lane1[:, :slots]
    mall[0, 1:2, 0:slots] = cols[...]
    mall[0, 2:3, 0:slots] = row_key
    wide = mall[0]
    tall_form = wide.T
    key_col, col_col, row_col = (tall_form[:slots, i:i + 1] for i in range(3))
    rank = jnp.sum((key_col < wide[0:1]).astype(jnp.int32), axis=0, keepdims=True)
    moves = jnp.where(rank[:, :slots] == lax.broadcasted_iota(jnp.int32, (slots, slots), 0), 1.0, 0.0)
    in_order = jnp.dot(moves.astype(jnp.bfloat16), tiles[0], preferred_element_type=jnp.float32)
    for m in range(BLOCK // 2):
        flat[:, m, :] = in_order[:, m * 2 * BLOCK:(m + 1) * 2 * BLOCK]
    first = lax.broadcasted_iota(jnp.int32, (BLOCK // 2, 2 * BLOCK), 1) < BLOCK
    for k in range(pairs):
        one, two = flat[2 * k], flat[2 * k + 1]
        rows2[k, pl.ds(0, BLOCK // 2, stride=2), :] = jnp.where(first, one, pltpu.roll(two, BLOCK, 1))
        rows2[k, pl.ds(1, BLOCK // 2, stride=2), :] = jnp.where(first, pltpu.roll(one, BLOCK, 1), two)
        tall[0, k] = rows2[k].astype(jnp.bfloat16)
    rank_col = jnp.where(pad == 0, rank, 0).T[:slots, 0:1]
    hit = rank_col == lane1

    def pull(values):
        return jnp.sum(jnp.where(hit, values, 0), axis=0, keepdims=True)

    upto = jnp.sum((row_col <= lane1).astype(jnp.int32), axis=0, keepdims=True)
    have = jnp.sum((row_col == lane1).astype(jnp.int32), axis=0, keepdims=True)
    for i, values in enumerate((pull(row_col), pull(col_col), jnp.maximum(upto - 1, 0), have)):
        mall[0, i:i + 1] = values
    to_smem = [pltpu.make_async_copy(mall.at[i], smeta.at[i], loc.at[i]) for i in range(n_col)]
    lane = lax.broadcasted_iota(jnp.int32, (16, 2 * BLOCK), 1)
    base = me_r * blocks
    pl.semaphore_wait(barrier, 2 + 1 + chips - 1)

    def x_ref(owner, c):
        return xall[c // X_CHUNKS].at[pl.ds(owner * blocks + c % X_CHUNKS * per, per)]

    def x_copy(owner, c, to, send, recv):
        return pltpu.make_async_remote_copy(
            src_ref=x_ref(owner, c), dst_ref=x_ref(owner, c), send_sem=send, recv_sem=recv,
            device_id=(to, me_c), device_id_type=MESH)

    def cross_to(k, c):
        return x_copy(me_r, c, ((chip + k) % chips) * 2 + core, cross_s.at[k - 1, c], cross_r.at[k - 1, c])

    def cross_from(k, c):
        owner = ((chip + chips - k) % chips) * 2 + core
        return x_copy(owner, c, owner, cross_s.at[k - 1, c], cross_r.at[k - 1, c])

    def sib_to(c):
        return x_copy(me_r, c, sibling, sib_s.at[c], sib_r.at[c])

    def sib_from(c):
        return x_copy(sibling, c, sibling, sib_s.at[c], sib_r.at[c])

    def fwd_to(k, c):
        owner = ((chip + chips - k) % chips) * 2 + core
        return x_copy(owner, c, sibling, fwd_s.at[k - 1, c], fwd_r.at[k - 1, c])

    def fwd_from(k, c):
        owner = ((chip + chips - k) % chips) * 2 + 1 - core
        return x_copy(owner, c, sibling, fwd_s.at[k - 1, c], fwd_r.at[k - 1, c])

    def ring_slots(d, t):
        return (t - 1, t) if d == 0 else ((n_col - t + 1) % n_col, n_col - t)

    def ring(d, t, h):
        a, b = ring_slots(d, t)
        cut = pl.ds(h * cut_pairs, cut_pairs)
        return pltpu.make_async_remote_copy(
            src_ref=tall.at[a, cut], dst_ref=tall.at[b, cut],
            send_sem=ring_s.at[d, t - 1, h], recv_sem=ring_r.at[d, t - 1, h],
            device_id=(me_r, nxt if d == 0 else prv), device_id_type=MESH)

    def meta(d, t):
        a, b = ring_slots(d, t)
        return pltpu.make_async_remote_copy(
            src_ref=mall.at[a], dst_ref=mall.at[b],
            send_sem=meta_s.at[d, t - 1], recv_sem=meta_r.at[d, t - 1],
            device_id=(me_r, nxt if d == 0 else prv), device_id_type=MESH)

    def ring_parts(t):
        if t < steps:
            return [(d, h) for h in range(HALVES) for d in (0, 1)], (0, 1)
        return [(0, 0), (1, 1)], (0,)

    def slot_of(q):
        return (q % 2) * ((q + 1) // 2) + (1 - q % 2) * ((n_col - q // 2) % n_col)

    def compute(q, arrays):
        lanes = slice(arrays[0] * orbs, (arrays[-1] + 1) * orbs)
        slot = slot_of(q)
        carry = None
        for g in range(slots // 4):
            r = [smeta[slot, 0, 4 * g + i] for i in range(4)]
            blank = jnp.zeros((BLOCK, 2 * BLOCK), jnp.bfloat16)
            grid = []
            for a in range(4):
                line = []
                for u in range(2):
                    if a < 2 * u:
                        line.append(blank)
                        continue
                    lead = lane < BLOCK
                    keep = lead if a == 2 * u else jnp.where(lead, r[2 * u], r[2 * u + 1]) == r[a]
                    keep = jnp.where(keep, 1.0, 0.0).astype(jnp.bfloat16)
                    mats = tall[slot, 2 * g + u].reshape(BLOCK // 16, 16, 2 * BLOCK)
                    line.append((mats * keep[None]).reshape(BLOCK, 2 * BLOCK))
                grid.append(jnp.concatenate(line, axis=1))
            where = [smeta[slot, 1, 4 * g + i] for i in range(4)]
            picked = jnp.concatenate([
                jnp.concatenate([xall[a][c] for c in where], axis=0) for a in arrays], axis=1)
            got = jnp.dot(jnp.concatenate(grid, axis=0), picked, preferred_element_type=jnp.float32)
            for a in range(4):
                one = got[a * BLOCK:(a + 1) * BLOCK]
                if carry is not None:
                    one = one + jnp.where(r[a] == before, carry, 0.0)
                sums[q * slots + 4 * g + a, :, lanes] = one
            carry, before = one, r[3]

    def add_rows(qs, begin):
        def row(b, carry):
            total = None if begin else acc[b]
            for q in qs:
                slot = slot_of(q)
                one = jnp.where(smeta[slot, 3, b] > 0, sums[q * slots + smeta[slot, 2, b]], 0.0)
                total = one if total is None else total + one
            acc[b] = total
            return carry

        lax.fori_loop(0, blocks, row, 0, unroll=4)

    def send_ring(t):
        pieces, metas = ring_parts(t)
        for d in metas:
            meta(d, t).start()
        for d, h in pieces:
            ring(d, t, h).start()

    def ring_event(t):
        pieces, metas = ring_parts(t)
        more, more_metas = ring_parts(t + 1) if t < steps else ((), ())
        for d in metas:
            meta(d, t).wait_recv()
            if d in more_metas:
                meta(d, t + 1).start()
        for d, h in pieces:
            ring(d, t, h).wait_recv()
            if (d, h) in more:
                ring(d, t + 1, h).start()
        for d in metas:
            to_smem[ring_slots(d, t)[1]].start()

    send_ring(1)
    for i, (a, c) in enumerate(x_parts):
        piece = (coef, direc)[a][:, c * part:(c + 1) * part].astype(jnp.float32).T.astype(jnp.bfloat16)
        xall[a][pl.ds(base + c * per, per)] = piece.reshape(per, BLOCK, orbs)
        for k in range(1, chips):
            cross_to(k, i).start()
        sib_to(i).start()
    to_smem[0].start()
    to_smem[0].wait()

    def shards(begin, end, arrays):
        def shard(q, carry):
            compute(q, arrays)
            return carry

        lax.fori_loop(begin, end, shard, 0)

    def cross_event(i):
        for k in range(1, chips):
            cross_from(k, i).wait_recv()
            fwd_to(k, i).start()

    def settle(a):
        for i in range(a * X_CHUNKS, (a + 1) * X_CHUNKS):
            sib_from(i).wait_recv()
            for k in range(1, chips):
                fwd_from(k, i).wait_recv()

    def list_here(t):
        for d in (0, 1):
            to_smem[ring_slots(d, t)[1]].wait()

    ring_event(1)
    for i in range(X_CHUNKS):
        cross_event(i)
    ring_event(2)
    settle(0)
    list_here(1)
    list_here(2)
    for i in range(X_CHUNKS, 2 * X_CHUNKS - 1):
        cross_event(i)
    shards(0, 5, (0,))
    for t in range(3, steps):
        ring_event(t)
    cross_event(2 * X_CHUNKS - 1)
    settle(1)
    shards(0, 5, (1,))
    for t in range(3, steps):
        list_here(t)
    shards(5, n_col - 1, (0, 1))
    add_rows(range(n_col - 1), True)
    ring_event(steps)
    to_smem[steps].wait()
    shards(n_col - 1, n_col, (0, 1))
    add_rows((n_col - 1,), False)

    for a, out in enumerate((out_c, out_d)):
        for m in range(basis // 256):
            out[:, m * 256:(m + 1) * 256] = acc[4 * m:4 * m + 4, :, a * orbs:(a + 1) * orbs].reshape(256, orbs).T.astype(jnp.bfloat16)

    for c in range(len(x_parts)):
        sib_to(c).wait_send()
        for k in range(1, chips):
            cross_to(k, c).wait_send()
            fwd_to(k, c).wait_send()
    for t in range(1, steps + 1):
        pieces, metas = ring_parts(t)
        for d in metas:
            meta(d, t).wait_send()
        for d, h in pieces:
            ring(d, t, h).wait_send()


def hand_over(a, b, out_a, out_b, held, came, gone):
    half = a.shape[0] // 2
    here, there = [], []
    for i, (src, dst) in enumerate(((a, out_a), (b, out_b))):
        for h in (0, 1):
            at = pl.ds(h * half, half)
            n = 2 * i + h
            here.append(pltpu.make_async_copy(src.at[at], held.at[n], came.at[n]))
            there.append(pltpu.make_async_copy(held.at[n], dst.at[at], gone.at[n]))
            here[-1].start()
    for one, two in zip(here, there):
        one.wait()
        two.start()
    for two in there:
        two.wait()


def local(n_row, n_col, coefs, direction, tiles, block_rows, block_cols, counts):
    slots = tiles.shape[1]
    orbs, basis = coefs.shape
    width = 2 * orbs
    chips, steps = n_row // 2, n_col // 2
    vmem = pl.BlockSpec(memory_space=pltpu.VMEM)
    dma = pltpu.SemaphoreType.DMA
    out = jax.ShapeDtypeStruct((orbs, basis), jnp.bfloat16)
    results = pl.pallas_call(
        functools.partial(kernel, n_row, n_col),
        out_shape=(out, out),
        in_specs=[vmem] * 5 + [pl.BlockSpec(memory_space=pltpu.SMEM)],
        out_specs=(vmem, vmem),
        scratch_shapes=[
            pltpu.VMEM((n_row * basis // BLOCK, BLOCK, orbs), jnp.bfloat16),
            pltpu.VMEM((n_row * basis // BLOCK, BLOCK, orbs), jnp.bfloat16),
            pltpu.VMEM((n_col, slots // 2, BLOCK, 2 * BLOCK), jnp.bfloat16),
            pltpu.VMEM((n_col, 8, 128), jnp.int32),
            pltpu.SMEM((n_col, 8, 128), jnp.int32),
            pltpu.VMEM((n_col * slots, BLOCK, width), jnp.float32),
            pltpu.VMEM((basis // BLOCK, BLOCK, width), jnp.float32),
            pltpu.VMEM((slots, BLOCK // 2, 2 * BLOCK), jnp.float32),
            pltpu.VMEM((slots // 2, BLOCK, 2 * BLOCK), jnp.float32),
            dma((2 * X_CHUNKS,)), dma((2 * X_CHUNKS,)),
            dma((chips - 1, 2 * X_CHUNKS)), dma((chips - 1, 2 * X_CHUNKS)),
            dma((chips - 1, 2 * X_CHUNKS)), dma((chips - 1, 2 * X_CHUNKS)),
            dma((2, steps, HALVES)), dma((2, steps, HALVES)),
            dma((2, steps)), dma((2, steps)),
            dma((n_col,)),
        ],
        compiler_params=pltpu.CompilerParams(
            collective_id=0, has_side_effects=True, vmem_limit_bytes=56 * 2**20),
        name="block_sparse_apply",
    )(coefs, direction, tiles, block_rows, block_cols, counts)
    return tuple(pl.pallas_call(
        hand_over,
        out_shape=(out, out),
        in_specs=[pl.BlockSpec(memory_space=pl.ANY)] * 2,
        out_specs=(pl.BlockSpec(memory_space=pl.ANY),) * 2,
        scratch_shapes=[pltpu.VMEM((4, orbs // 2, basis), jnp.bfloat16), dma((4,)), dma((4,))],
        name="hand_over",
    )(*results))


def solution(mesh):
    body = functools.partial(local, mesh.shape["row"], mesh.shape["col"])
    return jax.shard_map(
        body,
        mesh=mesh,
        in_specs=(
            P("col", "row"),
            P("col", "row"),
            P("row", "col", None),
            P("row", "col"),
            P("row", "col"),
            P("row", "col"),
        ),
        out_specs=(P("col", "row"), P("col", "row")),
        check_vma=False,
    )
```

```python
import functools

import jax
import jax.numpy as jnp
from jax import lax
from jax.experimental import pallas as pl
from jax.experimental.pallas import tpu as pltpu
from jax.sharding import PartitionSpec as P

BLOCK = 64
X_CHUNKS = 2
HALVES = 2
MESH = pl.DeviceIdType.MESH


def kernel(n_row, n_col, coef, direc, tiles, rows, cols, counts, out_c, out_d,
           x_coef, x_direc, tall, mall, smeta, sums, acc, flat, rows2,
           sib_s, sib_r, cross_s, cross_r, fwd_s, fwd_r, ring_s, ring_r, meta_s, meta_r, loc):
    orbs, basis = coef.shape
    width = 2 * orbs
    slots = rows.shape[1]
    blocks = basis // BLOCK
    pairs = slots // 2
    cut_pairs = pairs // HALVES
    chips = n_row // 2
    steps = n_col // 2
    part = basis // X_CHUNKS
    per = part // BLOCK
    xall = (x_coef, x_direc)
    x_parts = [(a, c) for a in (0, 1) for c in range(X_CHUNKS)]

    me_r, me_c = lax.axis_index("row"), lax.axis_index("col")
    chip, core = me_r // 2, me_r % 2
    sibling = chip * 2 + 1 - core
    turn = me_c % 2
    pos = me_c // 2 + turn * (n_col - 1 - 2 * (me_c // 2))

    def at_pos(p):
        side = p // steps
        return 2 * (p + side * (n_col - 1 - 2 * p)) + side

    nxt, prv = at_pos((pos + 1) % n_col), at_pos((pos + n_col - 1) % n_col)

    barrier = pltpu.get_barrier_semaphore()
    for c in (nxt, prv):
        pl.semaphore_signal(barrier, inc=1, device_id=(me_r, c), device_id_type=MESH)
    pl.semaphore_signal(barrier, inc=1, device_id=(sibling, me_c), device_id_type=MESH)
    for k in range(1, chips):
        pl.semaphore_signal(barrier, inc=1, device_id=(((chip + k) % chips) * 2 + core, me_c), device_id_type=MESH)

    lane = lax.broadcasted_iota(jnp.int32, (16, 2 * BLOCK), 1)
    base = me_r * blocks
    for a, c in x_parts:
        piece = (coef, direc)[a][:, c * part:(c + 1) * part].T
        xall[a][pl.ds(base + c * per, per)] = piece.reshape(per, BLOCK, orbs)
    pl.semaphore_wait(barrier, 2 + 1 + chips - 1)

    def x_ref(owner, c):
        return xall[c // X_CHUNKS].at[pl.ds(owner * blocks + c % X_CHUNKS * per, per)]

    def x_copy(owner, c, to, send, recv):
        return pltpu.make_async_remote_copy(
            src_ref=x_ref(owner, c), dst_ref=x_ref(owner, c), send_sem=send, recv_sem=recv,
            device_id=(to, me_c), device_id_type=MESH)

    def cross_to(k, c):
        return x_copy(me_r, c, ((chip + k) % chips) * 2 + core, cross_s.at[k - 1, c], cross_r.at[k - 1, c])

    def cross_from(k, c):
        owner = ((chip + chips - k) % chips) * 2 + core
        return x_copy(owner, c, owner, cross_s.at[k - 1, c], cross_r.at[k - 1, c])

    def sib_to(c):
        return x_copy(me_r, c, sibling, sib_s.at[c], sib_r.at[c])

    def sib_from(c):
        return x_copy(sibling, c, sibling, sib_s.at[c], sib_r.at[c])

    def fwd_to(k, c):
        owner = ((chip + chips - k) % chips) * 2 + core
        return x_copy(owner, c, sibling, fwd_s.at[k - 1, c], fwd_r.at[k - 1, c])

    def fwd_from(k, c):
        owner = ((chip + chips - k) % chips) * 2 + 1 - core
        return x_copy(owner, c, sibling, fwd_s.at[k - 1, c], fwd_r.at[k - 1, c])

    def ring_slots(d, t):
        return (t - 1, t) if d == 0 else ((n_col - t + 1) % n_col, n_col - t)

    def ring(d, t, h):
        a, b = ring_slots(d, t)
        cut = pl.ds(h * cut_pairs, cut_pairs)
        return pltpu.make_async_remote_copy(
            src_ref=tall.at[a, cut], dst_ref=tall.at[b, cut],
            send_sem=ring_s.at[d, t - 1, h], recv_sem=ring_r.at[d, t - 1, h],
            device_id=(me_r, nxt if d == 0 else prv), device_id_type=MESH)

    def meta(d, t):
        a, b = ring_slots(d, t)
        return pltpu.make_async_remote_copy(
            src_ref=mall.at[a], dst_ref=mall.at[b],
            send_sem=meta_s.at[d, t - 1], recv_sem=meta_r.at[d, t - 1],
            device_id=(me_r, nxt if d == 0 else prv), device_id_type=MESH)

    def ring_parts(t):
        if t < steps:
            return [(d, h) for h in range(HALVES) for d in (0, 1)], (0, 1)
        return [(0, 0), (1, 1)], (0,)

    def slot_of(q):
        return (q % 2) * ((q + 1) // 2) + (1 - q % 2) * ((n_col - q // 2) % n_col)

    def compute(q, arrays):
        lanes = slice(arrays[0] * orbs, (arrays[-1] + 1) * orbs)
        slot = slot_of(q)
        carry = None
        for g in range(slots // 4):
            r = [smeta[slot, 0, 4 * g + i] for i in range(4)]
            blank = jnp.zeros((BLOCK, 2 * BLOCK), jnp.bfloat16)
            grid = []
            for a in range(4):
                line = []
                for u in range(2):
                    if a < 2 * u:
                        line.append(blank)
                        continue
                    lead = lane < BLOCK
                    keep = lead if a == 2 * u else jnp.where(lead, r[2 * u], r[2 * u + 1]) == r[a]
                    keep = jnp.where(keep, 1.0, 0.0).astype(jnp.bfloat16)
                    mats = tall[slot, 2 * g + u].reshape(BLOCK // 16, 16, 2 * BLOCK)
                    line.append((mats * keep[None]).reshape(BLOCK, 2 * BLOCK))
                grid.append(jnp.concatenate(line, axis=1))
            where = [smeta[slot, 1, 4 * g + i] for i in range(4)]
            picked = jnp.concatenate([
                jnp.concatenate([xall[a][c] for c in where], axis=0) for a in arrays], axis=1)
            got = jnp.dot(jnp.concatenate(grid, axis=0), picked, preferred_element_type=jnp.float32)
            for a in range(4):
                one = got[a * BLOCK:(a + 1) * BLOCK]
                if carry is not None:
                    one = one + jnp.where(r[a] == before, carry, 0.0)
                sums[q * slots + 4 * g + a, :, lanes] = one
            carry, before = one, r[3]

    def add_rows(qs, begin):
        def row(b, carry):
            total = None if begin else acc[b]
            for q in qs:
                slot = slot_of(q)
                one = jnp.where(smeta[slot, 3, b] > 0, sums[q * slots + smeta[slot, 2, b]], 0.0)
                total = one if total is None else total + one
            acc[b] = total
            return carry

        lax.fori_loop(0, blocks, row, 0, unroll=4)

    def send_ring(t):
        pieces, metas = ring_parts(t)
        for d in metas:
            meta(d, t).start()
        for d, h in pieces:
            ring(d, t, h).start()

    def ring_event(t):
        pieces, metas = ring_parts(t)
        more, more_metas = ring_parts(t + 1) if t < steps else ((), ())
        for d in metas:
            meta(d, t).wait_recv()
            if d in more_metas:
                meta(d, t + 1).start()
        for d, h in pieces:
            ring(d, t, h).wait_recv()
            if (d, h) in more:
                ring(d, t + 1, h).start()
        for d in metas:
            to_smem[ring_slots(d, t)[1]].start()

    for i in range(len(x_parts)):
        for k in range(1, chips):
            cross_to(k, i).start()
        sib_to(i).start()

    lane1 = lax.broadcasted_iota(jnp.int32, (1, 128), 1)
    pad = lax.broadcasted_iota(jnp.int32, (8, 128), 0)
    row_key = jnp.where(lane1[:, :slots] < counts[0, 0], rows[...], blocks)
    mall[0] = jnp.zeros((8, 128), jnp.int32)
    mall[0, 0:1, 0:slots] = row_key * slots + lane1[:, :slots]
    mall[0, 1:2, 0:slots] = cols[...]
    mall[0, 2:3, 0:slots] = row_key
    wide = mall[0]
    tall_form = wide.T
    key_col, col_col, row_col = (tall_form[:slots, i:i + 1] for i in range(3))
    rank = jnp.sum((key_col < wide[0:1]).astype(jnp.int32), axis=0, keepdims=True)
    moves = jnp.where(rank[:, :slots] == lax.broadcasted_iota(jnp.int32, (slots, slots), 0), 1.0, 0.0)
    in_order = jnp.dot(moves.astype(jnp.bfloat16), tiles[0], preferred_element_type=jnp.float32)
    for m in range(BLOCK // 2):
        flat[:, m, :] = in_order[:, m * 2 * BLOCK:(m + 1) * 2 * BLOCK]
    first = lax.broadcasted_iota(jnp.int32, (BLOCK // 2, 2 * BLOCK), 1) < BLOCK
    for k in range(pairs):
        one, two = flat[2 * k], flat[2 * k + 1]
        rows2[k, pl.ds(0, BLOCK // 2, stride=2), :] = jnp.where(first, one, pltpu.roll(two, BLOCK, 1))
        rows2[k, pl.ds(1, BLOCK // 2, stride=2), :] = jnp.where(first, pltpu.roll(one, BLOCK, 1), two)
        tall[0, k] = rows2[k].astype(jnp.bfloat16)
    rank_col = jnp.where(pad == 0, rank, 0).T[:slots, 0:1]
    hit = rank_col == lane1

    def pull(values):
        return jnp.sum(jnp.where(hit, values, 0), axis=0, keepdims=True)

    upto = jnp.sum((row_col <= lane1).astype(jnp.int32), axis=0, keepdims=True)
    have = jnp.sum((row_col == lane1).astype(jnp.int32), axis=0, keepdims=True)
    for i, values in enumerate((pull(row_col), pull(col_col), jnp.maximum(upto - 1, 0), have)):
        mall[0, i:i + 1] = values
    to_smem = [pltpu.make_async_copy(mall.at[i], smeta.at[i], loc.at[i]) for i in range(n_col)]

    send_ring(1)
    to_smem[0].start()
    to_smem[0].wait()

    def shards(begin, end, arrays):
        def shard(q, carry):
            compute(q, arrays)
            return carry

        lax.fori_loop(begin, end, shard, 0)

    def cross_event(i):
        for k in range(1, chips):
            cross_from(k, i).wait_recv()
            fwd_to(k, i).start()

    def settle(a):
        for i in range(a * X_CHUNKS, (a + 1) * X_CHUNKS):
            sib_from(i).wait_recv()
            for k in range(1, chips):
                fwd_from(k, i).wait_recv()

    def list_here(t):
        for d in (0, 1):
            to_smem[ring_slots(d, t)[1]].wait()

    cross_event(0)
    ring_event(1)
    for i in range(1, X_CHUNKS):
        cross_event(i)
    settle(0)
    list_here(1)
    shards(0, 3, (0,))
    for i in range(X_CHUNKS, 2 * X_CHUNKS - 1):
        cross_event(i)
    ring_event(2)
    list_here(2)
    shards(3, 5, (0,))
    cross_event(2 * X_CHUNKS - 1)
    settle(1)
    shards(0, 2, (1,))
    for t in range(3, steps):
        ring_event(t)
    shards(2, 5, (1,))
    for t in range(3, steps):
        list_here(t)
    shards(5, n_col - 1, (0, 1))
    add_rows(range(n_col - 1), True)
    ring_event(steps)
    to_smem[steps].wait()
    shards(n_col - 1, n_col, (0, 1))
    add_rows((n_col - 1,), False)

    for a, out in enumerate((out_c, out_d)):
        for m in range(basis // 256):
            out[:, m * 256:(m + 1) * 256] = acc[4 * m:4 * m + 4, :, a * orbs:(a + 1) * orbs].reshape(256, orbs).astype(jnp.bfloat16).T

    for c in range(len(x_parts)):
        sib_to(c).wait_send()
        for k in range(1, chips):
            cross_to(k, c).wait_send()
            fwd_to(k, c).wait_send()
    for t in range(1, steps + 1):
        pieces, metas = ring_parts(t)
        for d in metas:
            meta(d, t).wait_send()
        for d, h in pieces:
            ring(d, t, h).wait_send()


def hand_over(a, b, out_a, out_b, held, came, gone):
    half = a.shape[0] // 2
    here, there = [], []
    for i, (src, dst) in enumerate(((a, out_a), (b, out_b))):
        for h in (0, 1):
            at = pl.ds(h * half, half)
            n = 2 * i + h
            here.append(pltpu.make_async_copy(src.at[at], held.at[n], came.at[n]))
            there.append(pltpu.make_async_copy(held.at[n], dst.at[at], gone.at[n]))
            here[-1].start()
    for one, two in zip(here, there):
        one.wait()
        two.start()
    for two in there:
        two.wait()


def local(n_row, n_col, coefs, direction, tiles, block_rows, block_cols, counts):
    slots = tiles.shape[1]
    orbs, basis = coefs.shape
    width = 2 * orbs
    chips, steps = n_row // 2, n_col // 2
    vmem = pl.BlockSpec(memory_space=pltpu.VMEM)
    dma = pltpu.SemaphoreType.DMA
    out = jax.ShapeDtypeStruct((orbs, basis), jnp.bfloat16)
    results = pl.pallas_call(
        functools.partial(kernel, n_row, n_col),
        out_shape=(out, out),
        in_specs=[vmem] * 5 + [pl.BlockSpec(memory_space=pltpu.SMEM)],
        out_specs=(vmem, vmem),
        scratch_shapes=[
            pltpu.VMEM((n_row * basis // BLOCK, BLOCK, orbs), jnp.bfloat16),
            pltpu.VMEM((n_row * basis // BLOCK, BLOCK, orbs), jnp.bfloat16),
            pltpu.VMEM((n_col, slots // 2, BLOCK, 2 * BLOCK), jnp.bfloat16),
            pltpu.VMEM((n_col, 8, 128), jnp.int32),
            pltpu.SMEM((n_col, 8, 128), jnp.int32),
            pltpu.VMEM((n_col * slots, BLOCK, width), jnp.float32),
            pltpu.VMEM((basis // BLOCK, BLOCK, width), jnp.float32),
            pltpu.VMEM((slots, BLOCK // 2, 2 * BLOCK), jnp.float32),
            pltpu.VMEM((slots // 2, BLOCK, 2 * BLOCK), jnp.float32),
            dma((2 * X_CHUNKS,)), dma((2 * X_CHUNKS,)),
            dma((chips - 1, 2 * X_CHUNKS)), dma((chips - 1, 2 * X_CHUNKS)),
            dma((chips - 1, 2 * X_CHUNKS)), dma((chips - 1, 2 * X_CHUNKS)),
            dma((2, steps, HALVES)), dma((2, steps, HALVES)),
            dma((2, steps)), dma((2, steps)),
            dma((n_col,)),
        ],
        compiler_params=pltpu.CompilerParams(
            collective_id=0, has_side_effects=True, vmem_limit_bytes=56 * 2**20),
        name="block_sparse_apply",
    )(coefs, direction, tiles, block_rows, block_cols, counts)
    return tuple(pl.pallas_call(
        hand_over,
        out_shape=(out, out),
        in_specs=[pl.BlockSpec(memory_space=pl.ANY)] * 2,
        out_specs=(pl.BlockSpec(memory_space=pl.ANY),) * 2,
        scratch_shapes=[pltpu.VMEM((4, orbs // 2, basis), jnp.bfloat16), dma((4,)), dma((4,))],
        name="hand_over",
    )(*results))


def solution(mesh):
    body = functools.partial(local, mesh.shape["row"], mesh.shape["col"])
    return jax.shard_map(
        body,
        mesh=mesh,
        in_specs=(
            P("col", "row"),
            P("col", "row"),
            P("row", "col", None),
            P("row", "col"),
            P("row", "col"),
            P("row", "col"),
        ),
        out_specs=(P("col", "row"), P("col", "row")),
        check_vma=False,
    )
```

```python
import functools

import jax
import jax.numpy as jnp
from jax import lax
from jax.experimental import pallas as pl
from jax.experimental.pallas import tpu as pltpu
from jax.sharding import PartitionSpec as P

BLOCK = 64
X_CHUNKS = 2
RING_CUTS = 4
MESH = pl.DeviceIdType.MESH


def kernel(n_row, n_col, coef, direc, tiles, rows, cols, counts, out_c, out_d,
           x_coef, x_direc, tall, mall, smeta, sums, acc, flat, rows2,
           sib_s, sib_r, cross_s, cross_r, fwd_s, fwd_r, ring_s, ring_r, meta_s, meta_r, loc):
    orbs, basis = coef.shape
    width = 2 * orbs
    slots = rows.shape[1]
    blocks = basis // BLOCK
    pairs = slots // 2
    cut_pairs = pairs // RING_CUTS
    chips = n_row // 2
    steps = n_col // 2
    part = basis // X_CHUNKS
    per = part // BLOCK
    xall = (x_coef, x_direc)
    x_parts = [(a, c) for a in (0, 1) for c in range(X_CHUNKS)]

    me_r, me_c = lax.axis_index("row"), lax.axis_index("col")
    chip, core = me_r // 2, me_r % 2
    sibling = chip * 2 + 1 - core
    turn = me_c % 2
    pos = me_c // 2 + turn * (n_col - 1 - 2 * (me_c // 2))

    def at_pos(p):
        side = p // steps
        return 2 * (p + side * (n_col - 1 - 2 * p)) + side

    nxt, prv = at_pos((pos + 1) % n_col), at_pos((pos + n_col - 1) % n_col)

    barrier = pltpu.get_barrier_semaphore()
    for c in (nxt, prv):
        pl.semaphore_signal(barrier, inc=1, device_id=(me_r, c), device_id_type=MESH)
    pl.semaphore_signal(barrier, inc=1, device_id=(sibling, me_c), device_id_type=MESH)
    for k in range(1, chips):
        pl.semaphore_signal(barrier, inc=1, device_id=(((chip + k) % chips) * 2 + core, me_c), device_id_type=MESH)

    lane1 = lax.broadcasted_iota(jnp.int32, (1, 128), 1)
    pad = lax.broadcasted_iota(jnp.int32, (8, 128), 0)
    row_key = jnp.where(lane1[:, :slots] < counts[0, 0], rows[...], blocks)
    mall[0] = jnp.zeros((8, 128), jnp.int32)
    mall[0, 0:1, 0:slots] = row_key * slots + lane1[:, :slots]
    mall[0, 1:2, 0:slots] = cols[...]
    mall[0, 2:3, 0:slots] = row_key
    wide = mall[0]
    tall_form = wide.T
    key_col, col_col, row_col = (tall_form[:slots, i:i + 1] for i in range(3))
    rank = jnp.sum((key_col < wide[0:1]).astype(jnp.int32), axis=0, keepdims=True)
    moves = jnp.where(rank[:, :slots] == lax.broadcasted_iota(jnp.int32, (slots, slots), 0), 1.0, 0.0)
    in_order = jnp.dot(moves.astype(jnp.bfloat16), tiles[0], preferred_element_type=jnp.float32)
    for m in range(BLOCK // 2):
        flat[:, m, :] = in_order[:, m * 2 * BLOCK:(m + 1) * 2 * BLOCK]
    first = lax.broadcasted_iota(jnp.int32, (BLOCK // 2, 2 * BLOCK), 1) < BLOCK
    for k in range(pairs):
        one, two = flat[2 * k], flat[2 * k + 1]
        rows2[k, pl.ds(0, BLOCK // 2, stride=2), :] = jnp.where(first, one, pltpu.roll(two, BLOCK, 1))
        rows2[k, pl.ds(1, BLOCK // 2, stride=2), :] = jnp.where(first, pltpu.roll(one, BLOCK, 1), two)
        tall[0, k] = rows2[k].astype(jnp.bfloat16)
    rank_col = jnp.where(pad == 0, rank, 0).T[:slots, 0:1]
    hit = rank_col == lane1

    def pull(values):
        return jnp.sum(jnp.where(hit, values, 0), axis=0, keepdims=True)

    upto = jnp.sum((row_col <= lane1).astype(jnp.int32), axis=0, keepdims=True)
    have = jnp.sum((row_col == lane1).astype(jnp.int32), axis=0, keepdims=True)
    for i, values in enumerate((pull(row_col), pull(col_col), jnp.maximum(upto - 1, 0), have)):
        mall[0, i:i + 1] = values
    to_smem = [pltpu.make_async_copy(mall.at[i], smeta.at[i], loc.at[i]) for i in range(n_col)]
    lane = lax.broadcasted_iota(jnp.int32, (16, 2 * BLOCK), 1)
    base = me_r * blocks
    pl.semaphore_wait(barrier, 2 + 1 + chips - 1)

    def x_ref(owner, c):
        return xall[c // X_CHUNKS].at[pl.ds(owner * blocks + c % X_CHUNKS * per, per)]

    def x_copy(owner, c, to, send, recv):
        return pltpu.make_async_remote_copy(
            src_ref=x_ref(owner, c), dst_ref=x_ref(owner, c), send_sem=send, recv_sem=recv,
            device_id=(to, me_c), device_id_type=MESH)

    def cross_to(k, c):
        return x_copy(me_r, c, ((chip + k) % chips) * 2 + core, cross_s.at[k - 1, c], cross_r.at[k - 1, c])

    def cross_from(k, c):
        owner = ((chip + chips - k) % chips) * 2 + core
        return x_copy(owner, c, owner, cross_s.at[k - 1, c], cross_r.at[k - 1, c])

    def sib_to(c):
        return x_copy(me_r, c, sibling, sib_s.at[c], sib_r.at[c])

    def sib_from(c):
        return x_copy(sibling, c, sibling, sib_s.at[c], sib_r.at[c])

    def fwd_to(k, c):
        owner = ((chip + chips - k) % chips) * 2 + core
        return x_copy(owner, c, sibling, fwd_s.at[k - 1, c], fwd_r.at[k - 1, c])

    def fwd_from(k, c):
        owner = ((chip + chips - k) % chips) * 2 + 1 - core
        return x_copy(owner, c, sibling, fwd_s.at[k - 1, c], fwd_r.at[k - 1, c])

    def ring_slots(d, t):
        return (t - 1, t) if d == 0 else ((n_col - t + 1) % n_col, n_col - t)

    def ring(d, t, h):
        a, b = ring_slots(d, t)
        cut = pl.ds(h * cut_pairs, cut_pairs)
        return pltpu.make_async_remote_copy(
            src_ref=tall.at[a, cut], dst_ref=tall.at[b, cut],
            send_sem=ring_s.at[d, t - 1, h], recv_sem=ring_r.at[d, t - 1, h],
            device_id=(me_r, nxt if d == 0 else prv), device_id_type=MESH)

    def meta(d, t):
        a, b = ring_slots(d, t)
        return pltpu.make_async_remote_copy(
            src_ref=mall.at[a], dst_ref=mall.at[b],
            send_sem=meta_s.at[d, t - 1], recv_sem=meta_r.at[d, t - 1],
            device_id=(me_r, nxt if d == 0 else prv), device_id_type=MESH)

    def ring_parts(t):
        if t < steps:
            return [(d, h) for h in range(RING_CUTS) for d in (0, 1)], (0, 1)
        return [(h % 2, h) for h in range(RING_CUTS)], (0,)

    def slot_of(q):
        return (q % 2) * ((q + 1) // 2) + (1 - q % 2) * ((n_col - q // 2) % n_col)

    def compute(q, arrays):
        lanes = slice(arrays[0] * orbs, (arrays[-1] + 1) * orbs)
        slot = slot_of(q)
        carry = None
        for g in range(slots // 4):
            r = [smeta[slot, 0, 4 * g + i] for i in range(4)]
            blank = jnp.zeros((BLOCK, 2 * BLOCK), jnp.bfloat16)
            grid = []
            for a in range(4):
                line = []
                for u in range(2):
                    if a < 2 * u:
                        line.append(blank)
                        continue
                    lead = lane < BLOCK
                    keep = lead if a == 2 * u else jnp.where(lead, r[2 * u], r[2 * u + 1]) == r[a]
                    keep = jnp.where(keep, 1.0, 0.0).astype(jnp.bfloat16)
                    mats = tall[slot, 2 * g + u].reshape(BLOCK // 16, 16, 2 * BLOCK)
                    line.append((mats * keep[None]).reshape(BLOCK, 2 * BLOCK))
                grid.append(jnp.concatenate(line, axis=1))
            where = [smeta[slot, 1, 4 * g + i] for i in range(4)]
            picked = jnp.concatenate([
                jnp.concatenate([xall[a][c] for c in where], axis=0) for a in arrays], axis=1)
            got = jnp.dot(jnp.concatenate(grid, axis=0), picked, preferred_element_type=jnp.float32)
            for a in range(4):
                one = got[a * BLOCK:(a + 1) * BLOCK]
                if carry is not None:
                    one = one + jnp.where(r[a] == before, carry, 0.0)
                sums[q * slots + 4 * g + a, :, lanes] = one
            carry, before = one, r[3]

    def add_rows(qs, begin):
        def row(b, carry):
            total = None if begin else acc[b]
            for q in qs:
                slot = slot_of(q)
                one = jnp.where(smeta[slot, 3, b] > 0, sums[q * slots + smeta[slot, 2, b]], 0.0)
                total = one if total is None else total + one
            acc[b] = total
            return carry

        lax.fori_loop(0, blocks, row, 0, unroll=4)

    def send_ring(t):
        pieces, metas = ring_parts(t)
        for d in metas:
            meta(d, t).start()
        for d, h in pieces:
            ring(d, t, h).start()

    def ring_event(t):
        pieces, metas = ring_parts(t)
        more, more_metas = ring_parts(t + 1) if t < steps else ((), ())
        for d in metas:
            meta(d, t).wait_recv()
            if d in more_metas:
                meta(d, t + 1).start()
        for d, h in pieces:
            ring(d, t, h).wait_recv()
            if (d, h) in more:
                ring(d, t + 1, h).start()
        for d in metas:
            to_smem[ring_slots(d, t)[1]].start()

    send_ring(1)
    for i, (a, c) in enumerate(x_parts):
        piece = (coef, direc)[a][:, c * part:(c + 1) * part].T
        xall[a][pl.ds(base + c * per, per)] = piece.reshape(per, BLOCK, orbs)
        for k in range(1, chips):
            cross_to(k, i).start()
        sib_to(i).start()
    to_smem[0].start()
    to_smem[0].wait()

    def shards(begin, end, arrays):
        def shard(q, carry):
            compute(q, arrays)
            return carry

        lax.fori_loop(begin, end, shard, 0)

    def cross_event(i):
        for k in range(1, chips):
            cross_from(k, i).wait_recv()
            fwd_to(k, i).start()

    def settle(a):
        for i in range(a * X_CHUNKS, (a + 1) * X_CHUNKS):
            sib_from(i).wait_recv()
            for k in range(1, chips):
                fwd_from(k, i).wait_recv()

    def list_here(t):
        for d in (0, 1):
            to_smem[ring_slots(d, t)[1]].wait()

    ring_event(1)
    for i in range(X_CHUNKS):
        cross_event(i)
    ring_event(2)
    settle(0)
    list_here(1)
    list_here(2)
    for i in range(X_CHUNKS, 2 * X_CHUNKS - 1):
        cross_event(i)
    shards(0, 3, (0,))
    for t in range(3, steps):
        ring_event(t)
    cross_event(2 * X_CHUNKS - 1)
    settle(1)
    shards(0, 3, (1,))
    for t in range(3, steps):
        list_here(t)
    shards(3, n_col - 1, (0, 1))
    add_rows(range(n_col - 1), True)
    ring_event(steps)
    to_smem[steps].wait()
    shards(n_col - 1, n_col, (0, 1))
    add_rows((n_col - 1,), False)

    for a, out in enumerate((out_c, out_d)):
        for m in range(basis // 256):
            out[:, m * 256:(m + 1) * 256] = acc[4 * m:4 * m + 4, :, a * orbs:(a + 1) * orbs].reshape(256, orbs).astype(jnp.bfloat16).T

    for c in range(len(x_parts)):
        sib_to(c).wait_send()
        for k in range(1, chips):
            cross_to(k, c).wait_send()
            fwd_to(k, c).wait_send()
    for t in range(1, steps + 1):
        pieces, metas = ring_parts(t)
        for d in metas:
            meta(d, t).wait_send()
        for d, h in pieces:
            ring(d, t, h).wait_send()


def hand_over(a, b, out_a, out_b, held, came, gone):
    half = a.shape[0] // 2
    here, there = [], []
    for i, (src, dst) in enumerate(((a, out_a), (b, out_b))):
        for h in (0, 1):
            at = pl.ds(h * half, half)
            n = 2 * i + h
            here.append(pltpu.make_async_copy(src.at[at], held.at[n], came.at[n]))
            there.append(pltpu.make_async_copy(held.at[n], dst.at[at], gone.at[n]))
            here[-1].start()
    for one, two in zip(here, there):
        one.wait()
        two.start()
    for two in there:
        two.wait()


def local(n_row, n_col, coefs, direction, tiles, block_rows, block_cols, counts):
    slots = tiles.shape[1]
    orbs, basis = coefs.shape
    width = 2 * orbs
    chips, steps = n_row // 2, n_col // 2
    vmem = pl.BlockSpec(memory_space=pltpu.VMEM)
    dma = pltpu.SemaphoreType.DMA
    out = jax.ShapeDtypeStruct((orbs, basis), jnp.bfloat16)
    results = pl.pallas_call(
        functools.partial(kernel, n_row, n_col),
        out_shape=(out, out),
        in_specs=[vmem] * 5 + [pl.BlockSpec(memory_space=pltpu.SMEM)],
        out_specs=(vmem, vmem),
        scratch_shapes=[
            pltpu.VMEM((n_row * basis // BLOCK, BLOCK, orbs), jnp.bfloat16),
            pltpu.VMEM((n_row * basis // BLOCK, BLOCK, orbs), jnp.bfloat16),
            pltpu.VMEM((n_col, slots // 2, BLOCK, 2 * BLOCK), jnp.bfloat16),
            pltpu.VMEM((n_col, 8, 128), jnp.int32),
            pltpu.SMEM((n_col, 8, 128), jnp.int32),
            pltpu.VMEM((n_col * slots, BLOCK, width), jnp.float32),
            pltpu.VMEM((basis // BLOCK, BLOCK, width), jnp.float32),
            pltpu.VMEM((slots, BLOCK // 2, 2 * BLOCK), jnp.float32),
            pltpu.VMEM((slots // 2, BLOCK, 2 * BLOCK), jnp.float32),
            dma((2 * X_CHUNKS,)), dma((2 * X_CHUNKS,)),
            dma((chips - 1, 2 * X_CHUNKS)), dma((chips - 1, 2 * X_CHUNKS)),
            dma((chips - 1, 2 * X_CHUNKS)), dma((chips - 1, 2 * X_CHUNKS)),
            dma((2, steps, RING_CUTS)), dma((2, steps, RING_CUTS)),
            dma((2, steps)), dma((2, steps)),
            dma((n_col,)),
        ],
        compiler_params=pltpu.CompilerParams(
            collective_id=0, has_side_effects=True, vmem_limit_bytes=56 * 2**20),
        name="block_sparse_apply",
    )(coefs, direction, tiles, block_rows, block_cols, counts)
    return tuple(pl.pallas_call(
        hand_over,
        out_shape=(out, out),
        in_specs=[pl.BlockSpec(memory_space=pl.ANY)] * 2,
        out_specs=(pl.BlockSpec(memory_space=pl.ANY),) * 2,
        scratch_shapes=[pltpu.VMEM((4, orbs // 2, basis), jnp.bfloat16), dma((4,)), dma((4,))],
        name="hand_over",
    )(*results))


def solution(mesh):
    body = functools.partial(local, mesh.shape["row"], mesh.shape["col"])
    return jax.shard_map(
        body,
        mesh=mesh,
        in_specs=(
            P("col", "row"),
            P("col", "row"),
            P("row", "col", None),
            P("row", "col"),
            P("row", "col"),
            P("row", "col"),
        ),
        out_specs=(P("col", "row"), P("col", "row")),
        check_vma=False,
    )
```
